32 devices in a mesh: grid: 8 (over z, y), band: 4 (over x, core).
Axes of the slice: x: 2, y: 2, z: 4, core: 2. Of those that a mesh axis runs over, the one named last changes fastest.
Arguments:
- orbitals: bfloat16 [4096, 4096], P(('band', 'grid')), may hold values from -6 to 6
- w_first: bfloat16 [4096, 1024], P(('band', 'grid')), may hold values from -0.09375 to 0.09375
- w_second: bfloat16 [4096, 1024], P(('band', 'grid')), may hold values from -0.09375 to 0.09375
- pivots: int32 [8, 4, 256], P('grid'), may hold values from 0 to 511, as said below
Outputs:
- chosen: bfloat16 [1024, 256], replicated
- quality: float32 [8, 256], P('grid')
The draws below stay inside these ranges and needn't reach their ends.
Inputs may be any that keep to these rules, and one draw needn't show every extreme that they name: Each list pivots[g, r, :] holds distinct values below 512 and contains 2 * 256 - 1; indices g that agree in all bits from bit r upward have equal lists in round r.
All inputs are finite; a program needn't handle non-finite values.
Results may differ from the reference program's by a relative error of at most 0.0026.
Values may be sent and summed in bfloat16 or wider, within the bound.
No kernel may reach another device: no remote copies, remote signals or barrier semaphores. Data moves between devices by JAX's collectives and lax.ppermute only.
A program may use at most 64 MiB of HBM per device.

```python
import jax
import jax.numpy as jnp

NB = 4096
SKETCH_WIDTH = 1024
C = 256
NG = 4096
ROUNDS = 4
N_GRID = 8


strengths = (0.9, 0.495, 0.272, 0.1497, 0.0823, 0.0453)


noise_level = 0.2


def draw_orbitals(key, part):
    key_rows, key_points, key_rough = jax.random.split(jax.random.fold_in(key, 4051), 3)
    profiles = len(strengths)
    row_factors = jax.random.normal(key_rows, (NB, profiles), jnp.float32)
    point_factors = jax.random.normal(key_points, (profiles, NG), jnp.float32)
    residue = jax.random.normal(key_rough, (NB, NG), jnp.float32)
    combined = noise_level * residue
    for profile in range(profiles):
        combined = combined + strengths[profile] * row_factors[:, profile:profile + 1] * point_factors[profile:profile + 1, :]
    return jnp.clip(combined, -6.0, 6.0).astype(jnp.bfloat16)


def draw_pivots(key, part):
    per_section = []
    for section in range(ROUNDS):

        def draw_list(group):
            subkey = jax.random.fold_in(jax.random.fold_in(key, 7919 + section), group)
            key_pick, key_order = jax.random.split(subkey)
            others = jax.random.permutation(key_pick, 2 * C - 1)[:C - 1].astype(jnp.int32)
            listed = jnp.concatenate([jnp.full((1,), 2 * C - 1, jnp.int32), others])
            return jax.random.permutation(key_order, listed)
        groups = jnp.arange(N_GRID, dtype=jnp.int32) >> section
        per_section.append(jax.vmap(draw_list)(groups))
    return jnp.stack(per_section, axis=1)


def block_levels(stream_key, extent, cuts, least, top_value):
    level = 1.0
    for position, shards_of in cuts:
        heights = jax.random.uniform(jax.random.fold_in(jax.random.fold_in(stream_key, 6), position), (shards_of,), jnp.float32, least / len(cuts), top_value / len(cuts))
        level = level * jnp.repeat(jnp.exp(heights), extent[position] // shards_of).reshape((-1,) + (1,) * (len(extent) - 1 - position))
    return level


def scatter_about(own_key, shape, deviation, bound, pieces=(), kind=jnp.bfloat16):
    entries = deviation * jax.random.normal(own_key, shape, jnp.float32)
    if pieces:
        entries = entries * block_levels(own_key, shape, pieces, -0.22, 0.18)
    return jnp.clip(entries, -bound, bound).astype(kind)


def setup_inputs(seed: int = 0) -> dict:
    splits = jax.random.split(jax.random.key(seed), 5)
    orbitals = draw_orbitals(jax.random.fold_in(splits[4], 71), 0)
    w_first = scatter_about(splits[1], (NB, SKETCH_WIDTH), NB ** -0.5, 0.09375, ((0, 32),))
    w_second = scatter_about(splits[2], (NB, SKETCH_WIDTH), NB ** -0.5, 0.09375, ((0, 32),))
    pivots = draw_pivots(jax.random.fold_in(splits[4], 71), 0)
    return {"orbitals": orbitals, "w_first": w_first, "w_second": w_second, "pivots": pivots}


ridge = 0.1

def log_pivots(chosen):
    widened_sketch = chosen.astype(jnp.float32)
    gram_product = jnp.einsum('vls,vli->vsi', widened_sketch, widened_sketch) / SKETCH_WIDTH
    gram_product = gram_product + ridge * jnp.eye(C, dtype=jnp.float32)
    cholesky_factor = jnp.linalg.cholesky(gram_product)
    return jnp.log(jnp.diagonal(cholesky_factor, axis1=1, axis2=2))

def reference(orbitals, w_first, w_second, pivots):
    sketch_first = jnp.dot(w_first.T.astype(jnp.float32), orbitals.astype(jnp.float32), preferred_element_type=jnp.float32)
    sketch_second = jnp.dot(w_second.T.astype(jnp.float32), orbitals.astype(jnp.float32), preferred_element_type=jnp.float32)
    pair_products = (sketch_first * sketch_second).astype(jnp.bfloat16)
    point_blocks = pair_products.reshape(SKETCH_WIDTH, N_GRID, 2 * C).transpose(1, 0, 2)
    chosen = jnp.take_along_axis(point_blocks, pivots[:, 0, None, :], axis=2)
    quality = log_pivots(chosen)
    positions = jnp.arange(N_GRID, dtype=jnp.int32)
    for section in range(1, ROUNDS):
        partner_bit = 1 << section - 1
        lower_set = chosen[positions - (positions & partner_bit)]
        upper_set = chosen[positions | partner_bit]
        merged = jnp.concatenate([lower_set, upper_set], axis=2)
        chosen = jnp.take_along_axis(merged, pivots[:, section, None, :], axis=2)
        quality = quality + log_pivots(chosen)
    return (chosen[0], quality)
```

```python
import functools

import jax
import jax.numpy as jnp
from jax import lax
from jax.experimental import pallas as pl
from jax.experimental.pallas import tpu as pltpu
from jax.sharding import PartitionSpec as P

ridge = 0.1
f32, bf16, f16 = jnp.float32, jnp.bfloat16, jnp.float16
step = 8
column_dims = (((0,), (0,)), ((), ()))


def bits_of(count):
    return count.bit_length() - 1


def exchange(block, axis, delta):
    count = lax.axis_size(axis)
    return lax.ppermute(block, axis, [(i, i ^ delta) for i in range(count)])


def reversed_bits(value, bits):
    out = 0
    for t in range(bits):
        out = out | ((value >> t) & 1) << (bits - 1 - t)
    return out


def select_kernel(where_ref, pivots_ref, orbitals_ref, out_ref):
    order = pivots_ref[0]
    width, kept = orbitals_ref.shape[1], order.shape[1]
    one_hot = (lax.broadcasted_iota(jnp.int32, (width, kept), 0) == order).astype(f32).astype(bf16)
    out_ref[0] = jnp.dot(orbitals_ref[...], one_hot, preferred_element_type=f32).astype(bf16)


def select_points(orbitals, orders, here):
    groups, _, kept = orders.shape
    rows, points = orbitals.shape
    width = points // groups
    high = bits_of(groups) - 1
    return pl.pallas_call(
        select_kernel,
        grid_spec=pltpu.PrefetchScalarGridSpec(
            num_scalar_prefetch=1,
            grid=(groups,),
            in_specs=[
                pl.BlockSpec((1, 1, kept), lambda d, w: (d, 0, 0)),
                pl.BlockSpec((rows, width), lambda d, w: (0, w[0] ^ d)),
            ],
            out_specs=pl.BlockSpec((1, rows, kept), lambda d, w: (d & 1, 0, reversed_bits(d >> 1, high))),
        ),
        out_shape=jax.ShapeDtypeStruct((2, rows, groups // 2 * kept), bf16),
    )(here[None], orders, orbitals)


def split3(v):
    a = v.astype(bf16)
    rest = v - a.astype(f32)
    b = rest.astype(bf16)
    c = (rest - b.astype(f32)).astype(bf16)
    return a, b, c


def pivots_kernel(sets, *refs):
    cands, out_ref, grams = refs[:sets], refs[sets], refs[sets + 1 :]
    rows, n = cands[0].shape
    diagonal = lax.broadcasted_iota(jnp.int32, (n, n), 0) == lax.broadcasted_iota(jnp.int32, (n, n), 1)
    shift = jnp.where(diagonal, f32(ridge), f32(0))
    for cand, gram in zip(cands, grams):
        product = lax.dot_general(cand[...], cand[...], column_dims, preferred_element_type=f32)
        gram[...] = product * f32(1 / rows) + shift
    out_ref[...] = jnp.zeros_like(out_ref)
    sublane = lax.broadcasted_iota(jnp.int32, (step, n), 0)
    lane = lax.broadcasted_iota(jnp.int32, (step, n), 1)
    below = lax.broadcasted_iota(jnp.int32, (step, 1), 0)

    def panel(k, carry):
        first = pl.multiple_of(k * step, step)
        on_diagonal = lane == first + sublane
        for q, gram in enumerate(grams):
            block = gram[pl.ds(first, step), :]
            corner = [
                jnp.sum(jnp.where(on_diagonal, block[i : i + 1, :], 0.0), axis=1, keepdims=True) for i in range(step)
            ]
            heads, inverses = [], []
            for j in range(step):
                head = corner[j][j : j + 1, :]
                inverse = 1.0 / head
                factor = jnp.where(below > j, corner[j] * inverse, 0.0)
                block = block - factor * block[j : j + 1, :]
                for c in range(j + 1, step):
                    corner[c] = corner[c] - factor * corner[c][j : j + 1, :]
                heads.append(head)
                inverses.append(inverse)
            column = jnp.concatenate(heads, axis=0)
            out_ref[q : q + 1, :] += jnp.sum(jnp.where(on_diagonal, column, 0.0), axis=0, keepdims=True)
            u1, u2, u3 = split3(block)
            v1, v2, v3 = split3(block * jnp.concatenate(inverses, axis=0))
            left = jnp.concatenate([v1, v1, v2, v2, v1, v3], axis=0)
            right = jnp.concatenate([u1, u2, u1, u2, u3, u1], axis=0)
            gram[...] -= lax.dot_general(left, right, column_dims, preferred_element_type=f32)
        return carry

    lax.fori_loop(0, n // step, panel, 0)
    out_ref[...] = 0.5 * jnp.log(out_ref[...])


def log_pivots(cands):
    sets, (rows, n) = len(cands), cands[0].shape
    return pl.pallas_call(
        functools.partial(pivots_kernel, sets),
        out_shape=jax.ShapeDtypeStruct((sets, n), f32),
        in_specs=[pl.BlockSpec(memory_space=pltpu.VMEM)] * sets,
        out_specs=pl.BlockSpec(memory_space=pltpu.VMEM),
        scratch_shapes=[pltpu.VMEM((n, n), f32)] * sets,
        compiler_params=pltpu.CompilerParams(vmem_limit_bytes=40 << 20),
    )(*cands)


def half_of(block, upper):
    size = block.shape[-1] // 2
    return lax.dynamic_slice_in_dim(block, upper * size, size, axis=block.ndim - 1)


def pack(block):
    block = block.reshape(-1, block.shape[-1])
    exponent = jnp.ceil(jnp.log2(jnp.maximum(jnp.max(jnp.abs(block)), f32(1e-30))))
    codes = (block * jnp.exp2(14.0 - exponent)).astype(f16)
    tag = jnp.full((16, codes.shape[-1]), exponent, f32).astype(f16)
    return jnp.concatenate([codes, tag], axis=0)


def unpack(codes, shape):
    return codes[:-16].astype(f32).reshape(shape) * jnp.exp2(codes[-1, 0].astype(f32) - 14.0)


def local(orbitals, w_first, w_second, pivots):
    here, place = lax.axis_index("grid"), lax.axis_index("band")
    grid_bits, band_bits = bits_of(lax.axis_size("grid")), bits_of(lax.axis_size("band"))
    order = pivots[0]
    kept = order.shape[1]

    orders = order[:1][None]
    for t in range(grid_bits):
        orders = jnp.concatenate([orders, exchange(orders, "grid", 1 << t)], axis=0)

    mixing = [jnp.stack([w_first, w_second])]
    for t in reversed(range(1, band_bits)):
        upper = place >> t & 1
        got = [exchange(half_of(m, 1 - upper), "band", 1 << t) for m in mixing]
        mixing = [half_of(m, upper) for m in mixing] + got
    mixing = mixing + [exchange(m, "grid", 1) for m in mixing]
    mixing = jnp.concatenate(mixing, axis=1)

    picked = select_points(orbitals, orders, here)
    own, got = picked[0], exchange(picked[1], "grid", 1)
    rows = [own]
    far = [got]
    for t in reversed(range(1, band_bits)):
        rows = rows + [exchange(m, "band", 1 << t) for m in rows]
        far = far + [exchange(m, "band", 1 << t) for m in far]
    rows = jnp.concatenate(rows + far, axis=0)

    mixes, points = [half_of(mixing, place & 1)], [rows]
    mixes.append(exchange(half_of(mixing, 1 - (place & 1)), "band", 1))
    points.append(exchange(rows, "band", 1))
    mixes, points = jnp.concatenate(mixes, axis=1), jnp.concatenate(points, axis=0)

    def partial(columns):
        return jnp.stack([lax.dot_general(m, columns, column_dims, preferred_element_type=f32) for m in mixes])

    size = points.shape[1]
    if grid_bits > 1:
        size = size // 2
        got = exchange(pack(partial(points[:, size:])), "grid", 2)
        sketch = partial(points[:, :size])
        sketch = sketch + unpack(got, sketch.shape)
    else:
        sketch = partial(points)
    for t in range(2, grid_bits):
        size = size // 2
        got = exchange(pack(sketch[..., size:]), "grid", 1 << t)
        sketch = sketch[..., :size]
        sketch = sketch + unpack(got, sketch.shape)
    chosen = (sketch[0] * sketch[1]).astype(bf16)

    def over_band(block):
        for t in reversed(range(band_bits)):
            got = exchange(block, "band", 1 << t)
            upper = place >> t & 1 == 1
            count = 1 << (band_bits - 1 - t)
            share = block.reshape((count, -1) + block.shape[1:])
            other = got.reshape(share.shape)
            low, high = jnp.where(upper, other, share), jnp.where(upper, share, other)
            block = jnp.concatenate([low, high], axis=1).reshape((-1,) + block.shape[1:])
        return block

    cands = [over_band(chosen)]
    index = lax.broadcasted_iota(jnp.int32, (kept, kept), 0)
    for section in range(1, grid_bits + 1):
        got = exchange(chosen, "grid", 1 << section - 1)
        upper = here >> section - 1 & 1
        mine = (index == order[section] - upper * kept).astype(bf16)
        other = (index == order[section] - (1 - upper) * kept).astype(bf16)
        chosen = jnp.dot(chosen, mine, preferred_element_type=f32) + jnp.dot(got, other, preferred_element_type=f32)
        chosen = chosen.astype(bf16)
        cands.append(over_band(chosen))
    quality = jnp.sum(log_pivots(cands), axis=0, keepdims=True)
    return cands[-1], quality


def solution(mesh):
    in_specs = (
        P(("band", "grid"), None),
        P(("band", "grid"), None),
        P(("band", "grid"), None),
        P("grid", None, None),
    )
    out_specs = (P(), P("grid", None))
    return jax.shard_map(local, mesh=mesh, in_specs=in_specs, out_specs=out_specs, check_vma=False)
```

```python
import functools

import jax
import jax.numpy as jnp
from jax import lax
from jax.experimental import pallas as pl
from jax.experimental.pallas import tpu as pltpu
from jax.sharding import PartitionSpec as P

ridge = 0.1
f32, bf16, f16 = jnp.float32, jnp.bfloat16, jnp.float16
step, height, lanes = 8, 32, 128
column_dims = (((0,), (0,)), ((), ()))


def bits_of(count):
    return count.bit_length() - 1


def exchange(block, axis, delta):
    count = lax.axis_size(axis)
    return lax.ppermute(block, axis, [(i, i ^ delta) for i in range(count)])


def reversed_bits(value, bits):
    out = 0
    for t in range(bits):
        out = out | ((value >> t) & 1) << (bits - 1 - t)
    return out


def select_kernel(where_ref, orders_ref, orbitals_ref, out_ref):
    kept = orders_ref.shape[2]
    width = orbitals_ref.shape[1] // 2
    index = lax.broadcasted_iota(jnp.int32, (width, kept), 0)
    for j in range(2):
        side = where_ref[0] & 1 ^ j
        one_hot = (index == orders_ref[side]).astype(f32).astype(bf16)
        columns = orbitals_ref[:, j * width : (j + 1) * width]
        out_ref[side, 0] = jnp.dot(columns, one_hot, preferred_element_type=f32).astype(bf16)


def select_points(orbitals, orders, here):
    groups, _, kept = orders.shape
    rows, points = orbitals.shape
    high = bits_of(groups) - 1
    parts = 2 if high else 1
    per_part = groups // 2 // parts

    def out_block(k, w):
        place = reversed_bits(k, high)
        return (0, place // per_part, 0, place % per_part)

    return pl.pallas_call(
        select_kernel,
        grid_spec=pltpu.PrefetchScalarGridSpec(
            num_scalar_prefetch=1,
            grid=(groups // 2,),
            in_specs=[
                pl.BlockSpec((2, 1, kept), lambda k, w: (k, 0, 0)),
                pl.BlockSpec((rows, 2 * points // groups), lambda k, w: (0, w[0] >> 1 ^ k)),
            ],
            out_specs=pl.BlockSpec((2, 1, rows, kept), out_block),
        ),
        out_shape=jax.ShapeDtypeStruct((2, parts, rows, per_part * kept), bf16),
    )(here[None], orders, orbitals)


def split3(v):
    a = v.astype(bf16)
    rest = v - a.astype(f32)
    b = rest.astype(bf16)
    c = (rest - b.astype(f32)).astype(bf16)
    return a, b, c


def eliminate(block, first):
    width = block.shape[1]
    lane = lax.broadcasted_iota(jnp.int32, (1, width), 1)
    on_diagonal = lax.broadcasted_iota(jnp.int32, (step, width), 1) - lax.broadcasted_iota(
        jnp.int32, (step, width), 0
    )
    done, scaled, diagonal = [], [], 0.0
    for corner in range(0, block.shape[0], step):
        below = lax.broadcasted_iota(jnp.int32, (block.shape[0], 1), 0)
        start = first + corner
        columns = [jnp.sum(jnp.where(lane == start + j, block, 0.0), axis=1, keepdims=True) for j in range(step)]
        heads, inverses = [], []
        for j in range(step):
            head = columns[j][j : j + 1, :]
            inverse = 1.0 / head
            factor = jnp.where(below > j, columns[j] * inverse, 0.0)
            block = block - factor * block[j : j + 1, :]
            for c in range(j + 1, step):
                columns[c] = columns[c] - factor * columns[c][j : j + 1, :]
            heads.append(head)
            inverses.append(inverse)
        heads = jnp.concatenate(heads, axis=0)
        diagonal = diagonal + jnp.sum(jnp.where(on_diagonal == start, heads, 0.0), axis=0, keepdims=True)
        done.append(block[:step])
        scaled.append(block[:step] * jnp.concatenate(inverses, axis=0))
        block = block[step:]
    return jnp.concatenate(done, axis=0), jnp.concatenate(scaled, axis=0), diagonal


def outer(scaled, rows):
    u1, u2, u3 = split3(rows)
    v1, v2, v3 = split3(scaled)
    left = jnp.concatenate([v1, v1, v2, v2, v1, v3], axis=0)
    right = jnp.concatenate([u1, u2, u1, u2, u3, u1], axis=0)
    return lax.dot_general(left, right, column_dims, preferred_element_type=f32)


def pivots_kernel(sets, *refs):
    cands, out_ref, grams = refs[:sets], refs[sets], refs[sets + 1 :]
    rows, n = cands[0].shape
    diagonal = lax.broadcasted_iota(jnp.int32, (n, n), 0) == lax.broadcasted_iota(jnp.int32, (n, n), 1)
    shift = jnp.where(diagonal, f32(ridge), f32(0))
    for cand, gram in zip(cands, grams):
        product = lax.dot_general(cand[...], cand[...], column_dims, preferred_element_type=f32)
        gram[...] = product * f32(1 / rows) + shift
    out_ref[...] = jnp.zeros_like(out_ref)
    for base in range(0, n, lanes):

        def panel(k, carry, base=base):
            first = pl.multiple_of(k * height, height)
            parts = [eliminate(gram[pl.ds(base + first, height), base:], first) for gram in grams]
            for q, (done, scaled, diagonal) in enumerate(parts):
                out_ref[q : q + 1, base:] += diagonal
                grams[q][base:, base:] -= outer(scaled, done)
            return carry

        lax.fori_loop(0, min(lanes, n - base) // height, panel, 0)
    out_ref[...] = 0.5 * jnp.log(out_ref[...])


def log_pivots(cands):
    sets, (rows, n) = len(cands), cands[0].shape
    return pl.pallas_call(
        functools.partial(pivots_kernel, sets),
        out_shape=jax.ShapeDtypeStruct((sets, n), f32),
        in_specs=[pl.BlockSpec(memory_space=pltpu.VMEM)] * sets,
        out_specs=pl.BlockSpec(memory_space=pltpu.VMEM),
        scratch_shapes=[pltpu.VMEM((n, n), f32)] * sets,
        compiler_params=pltpu.CompilerParams(vmem_limit_bytes=40 << 20),
    )(*cands)


def half_of(block, upper):
    size = block.shape[-1] // 2
    return lax.dynamic_slice_in_dim(block, upper * size, size, axis=block.ndim - 1)


def pack(block):
    block = block.reshape(-1, block.shape[-1])
    exponent = jnp.ceil(jnp.log2(jnp.maximum(jnp.max(jnp.abs(block)), f32(1e-30))))
    codes = (block * jnp.exp2(14.0 - exponent)).astype(f16)
    tag = jnp.full((16, codes.shape[-1]), exponent, f32).astype(f16)
    return jnp.concatenate([codes, tag], axis=0)


def unpack(codes, shape):
    return codes[:-16].astype(f32).reshape(shape) * jnp.exp2(codes[-1, 0].astype(f32) - 14.0)


def local(orbitals, w_first, w_second, pivots):
    here, place = lax.axis_index("grid"), lax.axis_index("band")
    grid_bits, band_bits = bits_of(lax.axis_size("grid")), bits_of(lax.axis_size("band"))
    order = pivots[0]
    kept = order.shape[1]

    mixing = [jnp.stack([w_first, w_second])]
    for t in reversed(range(1, band_bits)):
        upper = place >> t & 1
        got = [exchange(half_of(m, 1 - upper), "band", 1 << t) for m in mixing]
        mixing = [half_of(m, upper) for m in mixing] + got
    near = exchange(mixing[0], "grid", 1)

    orders = order[:1][None]
    for t in range(grid_bits):
        if t == grid_bits - 1:
            orders, mixing, near = lax.optimization_barrier((orders, mixing, near))
        orders = jnp.concatenate([orders, exchange(orders, "grid", 1 << t)], axis=0)
    mixing = jnp.concatenate(mixing + [near] + [exchange(m, "grid", 1) for m in mixing[1:]], axis=1)
    mixes = jnp.concatenate(
        [half_of(mixing, place & 1), exchange(half_of(mixing, 1 - (place & 1)), "band", 1)], axis=1
    )

    picked = select_points(orbitals, orders, here)
    picked, mixing = lax.optimization_barrier((picked, mixing))
    parts = []
    for part in reversed(range(picked.shape[1])):
        own, far = [picked[0, part]], [exchange(picked[1, part], "grid", 1)]
        for t in reversed(range(1, band_bits)):
            own = own + [exchange(m, "band", 1 << t) for m in own]
            far = far + [exchange(m, "band", 1 << t) for m in far]
        rows = jnp.concatenate(own + far, axis=0)
        parts.append(jnp.concatenate([rows, exchange(rows, "band", 1)], axis=0))

    def partial(columns):
        return jnp.stack([lax.dot_general(m, columns, column_dims, preferred_element_type=f32) for m in mixes])

    def swap(block, bit):
        return unpack(exchange(pack(block), "grid", 1 << bit), block.shape)

    def halves(block, bit):
        if bit + 1 >= grid_bits:
            return [block]
        size = block.shape[-1] // 2
        return [block[..., :size], block[..., size:]]

    if len(parts) > 1:
        go = [partial(columns) for columns in halves(parts[0], 1)]
        stay = [partial(columns) for columns in halves(parts[1], 1)]
        for t in range(1, grid_bits):
            got = [swap(block, t) for block in reversed(go)]
            total = [block + other for block, other in zip(stay, reversed(got))]
            if len(total) > 1:
                stay, go = halves(total[0], t + 1), halves(total[1], t + 1)
        sketch = total[0]
    else:
        sketch = partial(parts[0])
    chosen = (sketch[0] * sketch[1]).astype(bf16)

    def over_band(block):
        for t in reversed(range(band_bits)):
            got = exchange(block, "band", 1 << t)
            upper = place >> t & 1 == 1
            count = 1 << (band_bits - 1 - t)
            share = block.reshape((count, -1) + block.shape[1:])
            other = got.reshape(share.shape)
            low, high = jnp.where(upper, other, share), jnp.where(upper, share, other)
            block = jnp.concatenate([low, high], axis=1).reshape((-1,) + block.shape[1:])
        return block

    cands = [over_band(chosen)]
    index = lax.broadcasted_iota(jnp.int32, (kept, kept), 0)
    for section in range(1, grid_bits + 1):
        got = exchange(chosen, "grid", 1 << section - 1)
        upper = here >> section - 1 & 1
        mine = (index == order[section] - upper * kept).astype(bf16)
        other = (index == order[section] - (1 - upper) * kept).astype(bf16)
        chosen = jnp.dot(chosen, mine, preferred_element_type=f32) + jnp.dot(got, other, preferred_element_type=f32)
        chosen = chosen.astype(bf16)
        cands.append(over_band(chosen))
    quality = jnp.sum(log_pivots(cands), axis=0, keepdims=True)
    return cands[-1], quality


def solution(mesh):
    in_specs = (
        P(("band", "grid"), None),
        P(("band", "grid"), None),
        P(("band", "grid"), None),
        P("grid", None, None),
    )
    out_specs = (P(), P("grid", None))
    return jax.shard_map(local, mesh=mesh, in_specs=in_specs, out_specs=out_specs, check_vma=False)
```

```python
import functools

import jax
import jax.numpy as jnp
from jax import lax
from jax.experimental import pallas as pl
from jax.experimental.pallas import tpu as pltpu
from jax.sharding import PartitionSpec as P

ridge = 0.1
f32, bf16, f16 = jnp.float32, jnp.bfloat16, jnp.float16
step, height, lanes = 8, 32, 128
top, tag_rows = 14.0, 16
column_dims = (((0,), (0,)), ((), ()))


def bits_of(count):
    return count.bit_length() - 1


def exchange(block, axis, delta):
    count = lax.axis_size(axis)
    return lax.ppermute(block, axis, [(i, i ^ delta) for i in range(count)])


def reversed_bits(value, bits):
    out = 0
    for t in range(bits):
        out = out | ((value >> t) & 1) << (bits - 1 - t)
    return out


def pick_kernel(blocks_ref, orders_ref, array_ref, out_ref):
    index = lax.broadcasted_iota(jnp.int32, (array_ref.shape[1], orders_ref.shape[2]), 0)
    one_hot = (index == orders_ref[0]).astype(f32).astype(bf16)
    out_ref[...] = jnp.dot(array_ref[...], one_hot, preferred_element_type=f32).astype(bf16)


def pick(array, orders, blocks, width):
    count, _, kept = orders.shape
    rows = array.shape[0]
    return pl.pallas_call(
        pick_kernel,
        grid_spec=pltpu.PrefetchScalarGridSpec(
            num_scalar_prefetch=1,
            grid=(count,),
            in_specs=[
                pl.BlockSpec((1, 1, kept), lambda i, w: (i, 0, 0)),
                pl.BlockSpec((rows, width), lambda i, w: (0, w[i])),
            ],
            out_specs=pl.BlockSpec((rows, kept), lambda i, w: (0, i)),
        ),
        out_shape=jax.ShapeDtypeStruct((rows, count * kept), bf16),
    )(blocks, orders, array)


def split3(v):
    a = v.astype(bf16)
    rest = v - a.astype(f32)
    b = rest.astype(bf16)
    c = (rest - b.astype(f32)).astype(bf16)
    return a, b, c


def eliminate(block, first):
    width = block.shape[1]
    lane = lax.broadcasted_iota(jnp.int32, (1, width), 1)
    on_diagonal = lax.broadcasted_iota(jnp.int32, (step, width), 1) - lax.broadcasted_iota(
        jnp.int32, (step, width), 0
    )
    done, scaled, diagonal = [], [], 0.0
    for corner in range(0, block.shape[0], step):
        below = lax.broadcasted_iota(jnp.int32, (block.shape[0], 1), 0)
        start = first + corner
        columns = [jnp.sum(jnp.where(lane == start + j, block, 0.0), axis=1, keepdims=True) for j in range(step)]
        heads, inverses = [], []
        for j in range(step):
            head = columns[j][j : j + 1, :]
            inverse = 1.0 / head
            factor = jnp.where(below > j, columns[j] * inverse, 0.0)
            block = block - factor * block[j : j + 1, :]
            for c in range(j + 1, step):
                columns[c] = columns[c] - factor * columns[c][j : j + 1, :]
            heads.append(head)
            inverses.append(inverse)
        heads = jnp.concatenate(heads, axis=0)
        diagonal = diagonal + jnp.sum(jnp.where(on_diagonal == start, heads, 0.0), axis=0, keepdims=True)
        done.append(block[:step])
        scaled.append(block[:step] * jnp.concatenate(inverses, axis=0))
        block = block[step:]
    return jnp.concatenate(done, axis=0), jnp.concatenate(scaled, axis=0), diagonal


def outer(scaled, rows):
    u1, u2, u3 = split3(rows)
    v1, v2, v3 = split3(scaled)
    left = jnp.concatenate([v1, v1, v2, v2, v1, v3], axis=0)
    right = jnp.concatenate([u1, u2, u1, u2, u3, u1], axis=0)
    return lax.dot_general(left, right, column_dims, preferred_element_type=f32)


def pivots_kernel(sets, *refs):
    cands, out_ref, grams = refs[:sets], refs[sets], refs[sets + 1 :]
    rows, n = cands[0].shape
    diagonal = lax.broadcasted_iota(jnp.int32, (n, n), 0) == lax.broadcasted_iota(jnp.int32, (n, n), 1)
    shift = jnp.where(diagonal, f32(ridge), f32(0))
    for cand, gram in zip(cands, grams):
        product = lax.dot_general(cand[...], cand[...], column_dims, preferred_element_type=f32)
        gram[...] = product * f32(1 / rows) + shift
    out_ref[...] = jnp.zeros_like(out_ref)
    for base in range(0, n, lanes):

        def panel(k, carry, base=base):
            first = pl.multiple_of(k * height, height)
            parts = [eliminate(gram[pl.ds(base + first, height), base:], first) for gram in grams]
            for q, (done, scaled, diagonal) in enumerate(parts):
                out_ref[q : q + 1, base:] += diagonal
                grams[q][base:, base:] -= outer(scaled, done)
            return carry

        lax.fori_loop(0, min(lanes, n - base) // height, panel, 0)
    out_ref[...] = 0.5 * jnp.log(out_ref[...])


def log_pivots(cands):
    sets, (rows, n) = len(cands), cands[0].shape
    return pl.pallas_call(
        functools.partial(pivots_kernel, sets),
        out_shape=jax.ShapeDtypeStruct((sets, n), f32),
        in_specs=[pl.BlockSpec(memory_space=pltpu.VMEM)] * sets,
        out_specs=pl.BlockSpec(memory_space=pltpu.VMEM),
        scratch_shapes=[pltpu.VMEM((n, n), f32)] * sets,
        compiler_params=pltpu.CompilerParams(vmem_limit_bytes=40 << 20),
    )(*cands)


def half_of(block, upper):
    size = block.shape[1] // 2
    return lax.dynamic_slice_in_dim(block, upper * size, size, axis=1)


def sketch_kernel(mode, dots, plain, coded, *refs):
    refs, out_ref = refs[:-1], refs[-1]
    total = 0.0
    if dots:
        mix_ref, refs = refs[0], refs[1:]
        start = 0
        for points_ref in refs[:dots]:
            rows = points_ref.shape[0]
            total += jnp.dot(mix_ref[:, start : start + rows], points_ref[...], preferred_element_type=f32)
            start += rows
    for term in refs[dots : dots + plain]:
        total += term[...]
    for codes in refs[dots + plain :]:
        size = codes.shape[0] - tag_rows
        total += codes[:size, :] * jnp.exp2(codes[size : size + 1, :] - top)
    size = total.shape[0]
    if mode == "code":
        largest = jnp.maximum(jnp.max(jnp.abs(total), axis=(0, 1), keepdims=True), f32(1e-30))
        exponent = jnp.ceil(jnp.log2(largest))
        out_ref[:size, :] = total * jnp.exp2(top - exponent)
        out_ref[size:, :] = jnp.broadcast_to(exponent, (tag_rows, total.shape[1]))
    elif mode == "keep":
        out_ref[...] = total
    else:
        out_ref[...] = (total[: size // 2] * total[size // 2 :]).astype(bf16)


def sketch(mode, mix, points, plain, coded):
    size, columns = mix.shape[0], (points + plain + coded)[0].shape[1]
    rows, kind = {"code": (size + tag_rows, f32), "keep": (size, f32), "multiply": (size // 2, bf16)}[mode]
    operands = ([mix] + points if points else []) + plain + coded
    return pl.pallas_call(
        functools.partial(sketch_kernel, mode, len(points), len(plain), len(coded)),
        out_shape=jax.ShapeDtypeStruct((rows, columns), kind),
        in_specs=[pl.BlockSpec(memory_space=pltpu.VMEM)] * len(operands),
        out_specs=pl.BlockSpec(memory_space=pltpu.VMEM),
        compiler_params=pltpu.CompilerParams(vmem_limit_bytes=48 << 20),
    )(*operands)


def halves(block):
    size = (block[0] + block[1])[0].shape[1] // 2
    return [[[a[:, :size] for a in b] for b in block], [[a[:, size:] for a in b] for b in block]]


def local(orbitals, w_first, w_second, pivots):
    here, place = lax.axis_index("grid"), lax.axis_index("band")
    groups = lax.axis_size("grid")
    grid_bits, band_bits = bits_of(groups), bits_of(lax.axis_size("band"))
    order = pivots[0]
    kept = order.shape[1]
    width = orbitals.shape[1] // groups

    parts = 2 if grid_bits > 1 else 1
    count = groups // 2 // parts
    places = [[reversed_bits(p * count + i, grid_bits - 1) for i in range(count)] for p in range(parts)]
    raw = [
        lax.dynamic_slice_in_dim(orbitals, (here ^ 2 * k + 1) * width, width, axis=1) for k in places[-1]
    ]
    raw = exchange(jnp.concatenate(raw, axis=1), "grid", 1)

    mixing = [jnp.stack([w_first.T, w_second.T])]
    for t in reversed(range(1, band_bits)):
        upper = place >> t & 1
        got = [exchange(half_of(m, 1 - upper), "band", 1 << t) for m in mixing]
        mixing = [half_of(m, upper) for m in mixing] + got

    orders = order[:1][None]
    near = mixing[0]
    for t in reversed(range(1, grid_bits)):
        orders = jnp.stack([orders, exchange(orders, "grid", 1 << t)], axis=1).reshape((-1,) + orders.shape[1:])
        if t == grid_bits - 1:
            orders, near = lax.optimization_barrier((orders, near))
    near = exchange(near, "grid", 1)
    lists = [jnp.stack([orders[k] for k in p]) for p in places]

    def over_bands(block):
        blocks = [block]
        for t in reversed(range(1, band_bits)):
            blocks = blocks + [exchange(m, "band", 1 << t) for m in blocks]
        return blocks

    def names(p, side):
        return jnp.stack([here ^ 2 * k + side for k in places[p]])

    gathered = {}
    for p in reversed(range(parts)):
        own = over_bands(pick(orbitals, lists[p], names(p, 0), width))
        if p == parts - 1:
            far = pick(raw, lists[p], jnp.arange(count, dtype=jnp.int32), width)
        else:
            others = exchange(lists[p], "grid", 1)
            far = exchange(pick(orbitals, others, names(p, 1), width), "grid", 1)
        rows = jnp.concatenate(own + over_bands(far), axis=0)
        gathered[p] = [rows, exchange(rows, "band", 1)]

    mixing = jnp.concatenate(mixing + [near] + [exchange(m, "grid", 1) for m in mixing[1:]], axis=2)
    mixes = [half_of(mixing, place & 1), exchange(half_of(mixing, 1 - (place & 1)), "band", 1)]
    mix = jnp.concatenate(mixes, axis=2)
    mix = mix.reshape(-1, mix.shape[2])

    def swap(block, bit):
        codes = sketch("code", mix, block[0], [], block[1]).astype(f16)
        return exchange(codes, "grid", 1 << bit).astype(f32)

    stay = [gathered[0], []]
    if parts > 1:
        go = [gathered[1], []]
        for t in range(1, grid_bits - 1):
            got = [swap(block, t) for block in reversed(halves(go))]
            stay, go = [[points, codes + [new]] for (points, codes), new in zip(halves(stay), reversed(got))]
        kept_sum = sketch("keep", mix, stay[0], [], stay[1])
        chosen = sketch("multiply", mix, [], [kept_sum], [swap(go, grid_bits - 1)])
    else:
        chosen = sketch("multiply", mix, stay[0], [], [])

    def over_band(block):
        for t in reversed(range(band_bits)):
            got = exchange(block, "band", 1 << t)
            upper = place >> t & 1 == 1
            count = 1 << (band_bits - 1 - t)
            share = block.reshape((count, -1) + block.shape[1:])
            other = got.reshape(share.shape)
            low, high = jnp.where(upper, other, share), jnp.where(upper, share, other)
            block = jnp.concatenate([low, high], axis=1).reshape((-1,) + block.shape[1:])
        return block

    cands = [over_band(chosen)]
    index = lax.broadcasted_iota(jnp.int32, (kept, kept), 0)
    for section in range(1, grid_bits + 1):
        got = exchange(chosen, "grid", 1 << section - 1)
        upper = here >> section - 1 & 1
        mine = (index == order[section] - upper * kept).astype(bf16)
        other = (index == order[section] - (1 - upper) * kept).astype(bf16)
        chosen = jnp.dot(chosen, mine, preferred_element_type=f32) + jnp.dot(got, other, preferred_element_type=f32)
        chosen = chosen.astype(bf16)
        cands.append(over_band(chosen))
    quality = jnp.sum(log_pivots(cands), axis=0, keepdims=True)
    return cands[-1], quality


def solution(mesh):
    in_specs = (
        P(("band", "grid"), None),
        P(("band", "grid"), None),
        P(("band", "grid"), None),
        P("grid", None, None),
    )
    out_specs = (P(), P("grid", None))
    return jax.shard_map(local, mesh=mesh, in_specs=in_specs, out_specs=out_specs, check_vma=False)
```

```python
import functools

import jax
import jax.numpy as jnp
from jax import lax
from jax.experimental import pallas as pl
from jax.experimental.pallas import tpu as pltpu
from jax.sharding import PartitionSpec as P

ridge = 0.1
f32, bf16, f16 = jnp.float32, jnp.bfloat16, jnp.float16
step, height, lanes = 8, 32, 128
top, tag_rows = 14.0, 16
column_dims = (((0,), (0,)), ((), ()))


def bits_of(count):
    return count.bit_length() - 1


def exchange(block, axis, delta):
    count = lax.axis_size(axis)
    return lax.ppermute(block, axis, [(i, i ^ delta) for i in range(count)])


def reversed_bits(value, bits):
    out = 0
    for t in range(bits):
        out = out | ((value >> t) & 1) << (bits - 1 - t)
    return out


def pick(blocks, lists):
    out = []
    for block, listed in zip(blocks, lists):
        index = lax.broadcasted_iota(jnp.int32, (block.shape[1], listed.shape[0]), 0)
        one_hot = (index == listed).astype(bf16)
        out.append(jnp.dot(block, one_hot, preferred_element_type=f32).astype(bf16))
    return jnp.concatenate(out, axis=1)


def split3(v):
    a = v.astype(bf16)
    rest = v - a.astype(f32)
    b = rest.astype(bf16)
    c = (rest - b.astype(f32)).astype(bf16)
    return a, b, c


def eliminate(block, first):
    width = block.shape[1]
    lane = lax.broadcasted_iota(jnp.int32, (1, width), 1)
    on_diagonal = lax.broadcasted_iota(jnp.int32, (step, width), 1) - lax.broadcasted_iota(
        jnp.int32, (step, width), 0
    )
    done, scaled, diagonal = [], [], 0.0
    for corner in range(0, block.shape[0], step):
        below = lax.broadcasted_iota(jnp.int32, (block.shape[0], 1), 0)
        start = first + corner
        columns = [jnp.sum(jnp.where(lane == start + j, block, 0.0), axis=1, keepdims=True) for j in range(step)]
        heads, inverses = [], []
        for j in range(step):
            head = columns[j][j : j + 1, :]
            inverse = 1.0 / head
            factor = jnp.where(below > j, columns[j] * inverse, 0.0)
            block = block - factor * block[j : j + 1, :]
            for c in range(j + 1, step):
                columns[c] = columns[c] - factor * columns[c][j : j + 1, :]
            heads.append(head)
            inverses.append(inverse)
        heads = jnp.concatenate(heads, axis=0)
        diagonal = diagonal + jnp.sum(jnp.where(on_diagonal == start, heads, 0.0), axis=0, keepdims=True)
        done.append(block[:step])
        scaled.append(block[:step] * jnp.concatenate(inverses, axis=0))
        block = block[step:]
    return jnp.concatenate(done, axis=0), jnp.concatenate(scaled, axis=0), diagonal


def outer(scaled, rows):
    u1, u2, u3 = split3(rows)
    v1, v2, v3 = split3(scaled)
    left = jnp.concatenate([v1, v1, v2, v2, v1, v3], axis=0)
    right = jnp.concatenate([u1, u2, u1, u2, u3, u1], axis=0)
    return lax.dot_general(left, right, column_dims, preferred_element_type=f32)


def pivots_kernel(sets, *refs):
    cands, total_ref, out_ref, grams = refs[:sets], refs[sets], refs[sets + 1], refs[sets + 2 :]
    rows, n = cands[0].shape
    diagonal = lax.broadcasted_iota(jnp.int32, (n, n), 0) == lax.broadcasted_iota(jnp.int32, (n, n), 1)
    shift = jnp.where(diagonal, f32(ridge), f32(0))
    for cand, gram in zip(cands, grams):
        product = lax.dot_general(cand[...], cand[...], column_dims, preferred_element_type=f32)
        gram[...] = product * f32(1 / rows) + shift
    out_ref[...] = jnp.zeros_like(out_ref)
    for base in range(0, n, lanes):

        def panel(k, carry, base=base):
            first = pl.multiple_of(k * height, height)
            parts = [eliminate(gram[pl.ds(base + first, height), base:], first) for gram in grams]
            for q, (done, scaled, diagonal) in enumerate(parts):
                out_ref[q : q + 1, base:] += diagonal
                grams[q][base:, base:] -= outer(scaled, done)
            return carry

        lax.fori_loop(0, min(lanes, n - base) // height, panel, 0)
    total_ref[...] = jnp.sum(0.5 * jnp.log(out_ref[...]), axis=0, keepdims=True)


def log_pivots(cands):
    sets, (rows, n) = len(cands), cands[0].shape
    return pl.pallas_call(
        functools.partial(pivots_kernel, sets),
        out_shape=jax.ShapeDtypeStruct((1, n), f32),
        in_specs=[pl.BlockSpec(memory_space=pltpu.VMEM)] * sets,
        out_specs=pl.BlockSpec(memory_space=pltpu.VMEM),
        scratch_shapes=[pltpu.VMEM((sets, n), f32)] + [pltpu.VMEM((n, n), f32)] * sets,
        compiler_params=pltpu.CompilerParams(vmem_limit_bytes=40 << 20),
    )(*cands)


def half_of(block, upper):
    size = block.shape[1] // 2
    return lax.dynamic_slice_in_dim(block, upper * size, size, axis=1)


def sketch_kernel(mode, columns, starts, dots, plain, *refs):
    refs, out_ref = refs[:-1], refs[-1]
    total = 0.0
    if dots:
        mix_ref, refs = refs[0], refs[1:]
    views = [ref.at[:, start : start + columns] for ref, start in zip(refs, starts)]
    first = 0
    for points_ref in views[:dots]:
        rows = points_ref.shape[0]
        total += jnp.dot(mix_ref[:, first : first + rows], points_ref[...], preferred_element_type=f32)
        first += rows
    for term in views[dots : dots + plain]:
        total += term[...]
    for codes in views[dots + plain :]:
        size = codes.shape[0] - tag_rows
        total += codes[:size, :] * jnp.exp2(codes[size : size + 1, :] - top)
    size = total.shape[0]
    if mode == "code":
        largest = jnp.maximum(jnp.max(jnp.abs(total), axis=(0, 1), keepdims=True), f32(1e-30))
        exponent = jnp.ceil(jnp.log2(largest))
        out_ref[:size, :] = total * jnp.exp2(top - exponent)
        out_ref[size:, :] = jnp.broadcast_to(exponent, (tag_rows, total.shape[1]))
    elif mode == "keep":
        out_ref[...] = total
    else:
        out_ref[...] = (total[: size // 2] * total[size // 2 :]).astype(bf16)


def sketch(mode, columns, mix, points, plain, coded):
    size = mix.shape[0]
    rows, kind = {"code": (size + tag_rows, f32), "keep": (size, f32), "multiply": (size // 2, bf16)}[mode]
    terms = points + plain + coded
    operands = ([mix] if points else []) + [array for array, _ in terms]
    starts = [start for _, start in terms]
    return pl.pallas_call(
        functools.partial(sketch_kernel, mode, columns, starts, len(points), len(plain)),
        out_shape=jax.ShapeDtypeStruct((rows, columns), kind),
        in_specs=[pl.BlockSpec(memory_space=pltpu.VMEM)] * len(operands),
        out_specs=pl.BlockSpec(memory_space=pltpu.VMEM),
        compiler_params=pltpu.CompilerParams(vmem_limit_bytes=48 << 20),
    )(*operands)


def halves(block):
    size = block[0] // 2
    return [[size] + [[(a, first + shift) for a, first in terms] for terms in block[1:]] for shift in (0, size)]


def local(orbitals, w_first, w_second, pivots):
    here, place = lax.axis_index("grid"), lax.axis_index("band")
    groups = lax.axis_size("grid")
    grid_bits, band_bits = bits_of(groups), bits_of(lax.axis_size("band"))
    order = pivots[0]
    kept = order.shape[1]
    width = orbitals.shape[1] // groups

    orders = order[:1][None]
    orders = jnp.concatenate([orders, exchange(orders, "grid", 1)], axis=1)

    parts = 2 if grid_bits > 1 else 1
    count = groups // 2 // parts
    places = [[reversed_bits(p * count + i, grid_bits - 1) for i in range(count)] for p in range(parts)]

    def blocks_of(p, side):
        return [
            lax.dynamic_slice_in_dim(orbitals, (here ^ 2 * k + side) * width, width, axis=1) for k in places[p]
        ]

    raw = exchange(jnp.concatenate(blocks_of(parts - 1, 1), axis=1), "grid", 1)

    mixing = [jnp.stack([w_first.T, w_second.T])]
    for t in reversed(range(1, band_bits)):
        upper = place >> t & 1
        send = [half_of(m, 1 - upper) for m in mixing]
        orders, send = lax.optimization_barrier((orders, send))
        mixing = [half_of(m, upper) for m in mixing] + [exchange(m, "band", 1 << t) for m in send]
    near = mixing[0]
    for t in reversed(range(1, grid_bits)):
        orders = jnp.stack([orders, exchange(orders, "grid", 1 << t)], axis=1).reshape((-1,) + orders.shape[1:])
        if t == grid_bits - 1:
            orders, near = lax.optimization_barrier((orders, near))
    near = [near] + mixing[1:]
    near = [exchange(m, "grid", 1) for m in near]

    def over_bands(block):
        blocks = [block]
        for t in reversed(range(1, band_bits)):
            blocks = blocks + [exchange(m, "band", 1 << t) for m in blocks]
        return blocks

    def lists_of(p, side):
        return [orders[k, side] for k in places[p]]

    gathered = {}
    for p in reversed(range(parts)):
        own = over_bands(pick(blocks_of(p, 0), lists_of(p, 0)))
        if p == parts - 1:
            far = pick([raw[:, i * width : (i + 1) * width] for i in range(count)], lists_of(p, 0))
            orders, far = lax.optimization_barrier((orders, far))
        else:
            far = exchange(pick(blocks_of(p, 1), lists_of(p, 1)), "grid", 1)
        rows = jnp.concatenate(own + over_bands(far), axis=0)
        gathered[p] = [rows, exchange(rows, "band", 1)]

    mixing = jnp.concatenate(mixing + near, axis=2)
    mixes = [half_of(mixing, place & 1), exchange(half_of(mixing, 1 - (place & 1)), "band", 1)]
    mix = jnp.concatenate(mixes, axis=2)
    mix = mix.reshape(-1, mix.shape[2])

    def swap(block, bit):
        columns, points, codes = block
        new = sketch("code", columns, mix, points, [], codes).astype(f16)
        return exchange(new, "grid", 1 << bit).astype(f32), 0

    stay = [count * kept, [(rows, 0) for rows in gathered[0]], []]
    if parts > 1:
        go = [count * kept, [(rows, 0) for rows in gathered[1]], []]
        for t in range(1, grid_bits - 1):
            got = [swap(block, t) for block in reversed(halves(go))]
            stay, go = [
                [columns, points, codes + [new]] for (columns, points, codes), new in zip(halves(stay), reversed(got))
            ]
        held = sketch("keep", kept, mix, stay[1], [], stay[2])
        chosen = sketch("multiply", kept, mix, [], [(held, 0)], [swap(go, grid_bits - 1)])
    else:
        chosen = sketch("multiply", kept, mix, stay[1], [], [])

    def over_band(block):
        for t in reversed(range(band_bits)):
            got = exchange(block, "band", 1 << t)
            upper = place >> t & 1 == 1
            count = 1 << (band_bits - 1 - t)
            share = block.reshape((count, -1) + block.shape[1:])
            other = got.reshape(share.shape)
            low, high = jnp.where(upper, other, share), jnp.where(upper, share, other)
            block = jnp.concatenate([low, high], axis=1).reshape((-1,) + block.shape[1:])
        return block

    cands = [over_band(chosen)]
    index = lax.broadcasted_iota(jnp.int32, (kept, kept), 0)
    for section in range(1, grid_bits + 1):
        got = exchange(chosen, "grid", 1 << section - 1)
        upper = here >> section - 1 & 1
        mine = (index == order[section] - upper * kept).astype(bf16)
        other = (index == order[section] - (1 - upper) * kept).astype(bf16)
        chosen = jnp.dot(chosen, mine, preferred_element_type=f32) + jnp.dot(got, other, preferred_element_type=f32)
        chosen = chosen.astype(bf16)
        cands.append(over_band(chosen))
    return cands[-1], log_pivots(cands)


def solution(mesh):
    in_specs = (
        P(("band", "grid"), None),
        P(("band", "grid"), None),
        P(("band", "grid"), None),
        P("grid", None, None),
    )
    out_specs = (P(), P("grid", None))
    return jax.shard_map(local, mesh=mesh, in_specs=in_specs, out_specs=out_specs, check_vma=False)
```

```python
import functools

import jax
import jax.numpy as jnp
from jax import lax
from jax.experimental import pallas as pl
from jax.experimental.pallas import tpu as pltpu
from jax.sharding import PartitionSpec as P

ridge = 0.1
f32, bf16, f16 = jnp.float32, jnp.bfloat16, jnp.float16
step, height, lanes = 8, 32, 128
top, tag_rows = 14.0, 16
column_dims = (((0,), (0,)), ((), ()))


def bits_of(count):
    return count.bit_length() - 1


def exchange(block, axis, delta):
    count = lax.axis_size(axis)
    return lax.ppermute(block, axis, [(i, i ^ delta) for i in range(count)])


def reversed_bits(value, bits):
    out = 0
    for t in range(bits):
        out = out | ((value >> t) & 1) << (bits - 1 - t)
    return out


def pick(blocks, lists):
    out = []
    for block, listed in zip(blocks, lists):
        index = lax.broadcasted_iota(jnp.int32, (block.shape[1], listed.shape[0]), 0)
        one_hot = (index == listed).astype(bf16)
        out.append(jnp.dot(block, one_hot, preferred_element_type=f32).astype(bf16))
    return jnp.concatenate(out, axis=1)


def split3(v):
    a = v.astype(bf16)
    rest = v - a.astype(f32)
    b = rest.astype(bf16)
    c = (rest - b.astype(f32)).astype(bf16)
    return a, b, c


def eliminate(block, first):
    width = block.shape[1]
    lane = lax.broadcasted_iota(jnp.int32, (1, width), 1)
    on_diagonal = lax.broadcasted_iota(jnp.int32, (step, width), 1) - lax.broadcasted_iota(
        jnp.int32, (step, width), 0
    )
    done, scaled, diagonal = [], [], 0.0
    for corner in range(0, block.shape[0], step):
        below = lax.broadcasted_iota(jnp.int32, (block.shape[0], 1), 0)
        start = first + corner
        columns = [jnp.sum(jnp.where(lane == start + j, block, 0.0), axis=1, keepdims=True) for j in range(step)]
        heads, inverses = [], []
        for j in range(step):
            head = columns[j][j : j + 1, :]
            inverse = 1.0 / head
            factor = jnp.where(below > j, columns[j] * inverse, 0.0)
            block = block - factor * block[j : j + 1, :]
            for c in range(j + 1, step):
                columns[c] = columns[c] - factor * columns[c][j : j + 1, :]
            heads.append(head)
            inverses.append(inverse)
        heads = jnp.concatenate(heads, axis=0)
        diagonal = diagonal + jnp.sum(jnp.where(on_diagonal == start, heads, 0.0), axis=0, keepdims=True)
        done.append(block[:step])
        scaled.append(block[:step] * jnp.concatenate(inverses, axis=0))
        block = block[step:]
    return jnp.concatenate(done, axis=0), jnp.concatenate(scaled, axis=0), diagonal


def outer(scaled, rows):
    u1, u2, u3 = split3(rows)
    v1, v2, v3 = split3(scaled)
    left = jnp.concatenate([v1, v1, v2, v2, v1, v3], axis=0)
    right = jnp.concatenate([u1, u2, u1, u2, u3, u1], axis=0)
    return lax.dot_general(left, right, column_dims, preferred_element_type=f32)


def pivots_kernel(sets, *refs):
    cands, total_ref, out_ref, grams = refs[:sets], refs[sets], refs[sets + 1], refs[sets + 2 :]
    rows, n = cands[0].shape
    diagonal = lax.broadcasted_iota(jnp.int32, (n, n), 0) == lax.broadcasted_iota(jnp.int32, (n, n), 1)
    shift = jnp.where(diagonal, f32(ridge), f32(0))
    for cand, gram in zip(cands, grams):
        product = lax.dot_general(cand[...], cand[...], column_dims, preferred_element_type=f32)
        gram[...] = product * f32(1 / rows) + shift
    out_ref[...] = jnp.zeros_like(out_ref)
    for base in range(0, n, lanes):

        def panel(k, carry, base=base):
            first = pl.multiple_of(k * height, height)
            parts = [eliminate(gram[pl.ds(base + first, height), base:], first) for gram in grams]
            for q, (done, scaled, diagonal) in enumerate(parts):
                out_ref[q : q + 1, base:] += diagonal
                grams[q][base:, base:] -= outer(scaled, done)
            return carry

        lax.fori_loop(0, min(lanes, n - base) // height, panel, 0)
    total_ref[...] = jnp.sum(0.5 * jnp.log(out_ref[...]), axis=0, keepdims=True)


def log_pivots(cands):
    sets, (rows, n) = len(cands), cands[0].shape
    return pl.pallas_call(
        functools.partial(pivots_kernel, sets),
        out_shape=jax.ShapeDtypeStruct((1, n), f32),
        in_specs=[pl.BlockSpec(memory_space=pltpu.VMEM)] * sets,
        out_specs=pl.BlockSpec(memory_space=pltpu.VMEM),
        scratch_shapes=[pltpu.VMEM((sets, n), f32)] + [pltpu.VMEM((n, n), f32)] * sets,
        compiler_params=pltpu.CompilerParams(vmem_limit_bytes=40 << 20),
    )(*cands)


def half_of(block, upper):
    size = block.shape[1] // 2
    return lax.dynamic_slice_in_dim(block, upper * size, size, axis=1)


def sketch_kernel(mode, columns, starts, dots, plain, *refs):
    refs, out_ref = refs[:-1], refs[-1]
    total = 0.0
    mixes, refs = refs[:dots], refs[dots:]
    views = [ref.at[:, start : start + columns] for ref, start in zip(refs, starts)]
    for mix_ref, points_ref in zip(mixes, views):
        total += jnp.dot(mix_ref[...], points_ref[...], preferred_element_type=f32)
    for term in views[dots : dots + plain]:
        total += term[...]
    for codes in views[dots + plain :]:
        size = codes.shape[0] - tag_rows
        total += codes[:size, :] * jnp.exp2(codes[size : size + 1, :] - top)
    size = total.shape[0]
    if mode == "code":
        largest = jnp.maximum(jnp.max(jnp.abs(total), axis=(0, 1), keepdims=True), f32(1e-30))
        exponent = jnp.ceil(jnp.log2(largest))
        out_ref[:size, :] = total * jnp.exp2(top - exponent)
        out_ref[size:, :] = jnp.broadcast_to(exponent, (tag_rows, total.shape[1]))
    elif mode == "keep":
        out_ref[...] = total
    else:
        out_ref[...] = (total[: size // 2] * total[size // 2 :]).astype(bf16)


def sketch(mode, columns, mixes, points, plain, coded):
    size = mixes[0].shape[0]
    rows, kind = {"code": (size + tag_rows, f32), "keep": (size, f32), "multiply": (size // 2, bf16)}[mode]
    terms = points + plain + coded
    operands = mixes[: len(points)] + [array for array, _ in terms]
    starts = [start for _, start in terms]
    return pl.pallas_call(
        functools.partial(sketch_kernel, mode, columns, starts, len(points), len(plain)),
        out_shape=jax.ShapeDtypeStruct((rows, columns), kind),
        in_specs=[pl.BlockSpec(memory_space=pltpu.VMEM)] * len(operands),
        out_specs=pl.BlockSpec(memory_space=pltpu.VMEM),
        compiler_params=pltpu.CompilerParams(vmem_limit_bytes=48 << 20),
    )(*operands)


def halves(block):
    size = block[0] // 2
    return [[size] + [[(a, first + shift) for a, first in terms] for terms in block[1:]] for shift in (0, size)]


def local(orbitals, w_first, w_second, pivots):
    here, place = lax.axis_index("grid"), lax.axis_index("band")
    groups = lax.axis_size("grid")
    grid_bits, band_bits = bits_of(groups), bits_of(lax.axis_size("band"))
    order = pivots[0]
    kept = order.shape[1]
    width = orbitals.shape[1] // groups

    parts = 2 if grid_bits > 1 else 1
    count = groups // 2 // parts
    places = [[reversed_bits(p * count + i, grid_bits - 1) for i in range(count)] for p in range(parts)]

    def blocks_of(p, side):
        return [
            lax.dynamic_slice_in_dim(orbitals, (here ^ 2 * k + side) * width, width, axis=1) for k in places[p]
        ]

    raw = exchange(jnp.concatenate(blocks_of(parts - 1, 1), axis=1), "grid", 1)

    mixing = [jnp.stack([w_first.T, w_second.T])]
    for t in reversed(range(1, band_bits)):
        upper = place >> t & 1
        got = [exchange(half_of(m, 1 - upper), "band", 1 << t) for m in mixing]
        mixing = [half_of(m, upper) for m in mixing] + got
    near = mixing[0]

    orders = order[:1]
    for t in reversed(range(1, grid_bits)):
        if t == 1:
            orders, raw, near, mixing = lax.optimization_barrier((orders, raw, near, mixing))
        orders = jnp.stack([orders, exchange(orders, "grid", 1 << t)], axis=1).reshape(-1, kept)
    near = [near] + mixing[1:]
    near = [exchange(m, "grid", 1) for m in near]

    def over_bands(block):
        blocks = [block]
        for t in reversed(range(1, band_bits)):
            blocks = blocks + [exchange(m, "band", 1 << t) for m in blocks]
        return blocks

    def lists_of(p):
        return jnp.stack([orders[k] for k in places[p]])

    gathered = {}
    for p in reversed(range(parts)):
        listed = lists_of(p)
        own = over_bands(pick(blocks_of(p, 0), listed))
        if p == parts - 1:
            far = pick([raw[:, i * width : (i + 1) * width] for i in range(count)], listed)
            orders, far = lax.optimization_barrier((orders, far))
        else:
            far = exchange(pick(blocks_of(p, 1), exchange(listed, "grid", 1)), "grid", 1)
        rows = jnp.concatenate(own + over_bands(far), axis=0)
        gathered[p] = [rows, exchange(rows, "band", 1)]

    mixing = jnp.concatenate(mixing + near, axis=2)
    mixes = [half_of(mixing, place & 1), exchange(half_of(mixing, 1 - (place & 1)), "band", 1)]
    mixes = [m.reshape(-1, m.shape[2]) for m in mixes]

    def swap(block, bit):
        columns, points, codes = block
        new = sketch("code", columns, mixes, points, [], codes).astype(f16)
        return exchange(new, "grid", 1 << bit).astype(f32), 0

    stay = [count * kept, [(rows, 0) for rows in gathered[0]], []]
    if parts > 1:
        go = [count * kept, [(rows, 0) for rows in gathered[1]], []]
        for t in range(1, grid_bits - 1):
            got = [swap(block, t) for block in reversed(halves(go))]
            stay, go = [
                [columns, points, codes + [new]] for (columns, points, codes), new in zip(halves(stay), reversed(got))
            ]
        held = sketch("keep", kept, mixes, stay[1], [], stay[2])
        chosen = sketch("multiply", kept, mixes, [], [(held, 0)], [swap(go, grid_bits - 1)])
    else:
        chosen = sketch("multiply", kept, mixes, stay[1], [], [])

    def over_band(block):
        for t in reversed(range(band_bits)):
            got = exchange(block, "band", 1 << t)
            upper = place >> t & 1 == 1
            count = 1 << (band_bits - 1 - t)
            share = block.reshape((count, -1) + block.shape[1:])
            other = got.reshape(share.shape)
            low, high = jnp.where(upper, other, share), jnp.where(upper, share, other)
            block = jnp.concatenate([low, high], axis=1).reshape((-1,) + block.shape[1:])
        return block

    cands = [over_band(chosen)]
    index = lax.broadcasted_iota(jnp.int32, (kept, kept), 0)
    for section in range(1, grid_bits + 1):
        got = exchange(chosen, "grid", 1 << section - 1)
        upper = here >> section - 1 & 1
        mine = (index == order[section] - upper * kept).astype(bf16)
        other = (index == order[section] - (1 - upper) * kept).astype(bf16)
        chosen = jnp.dot(chosen, mine, preferred_element_type=f32) + jnp.dot(got, other, preferred_element_type=f32)
        chosen = chosen.astype(bf16)
        cands.append(over_band(chosen))
    return cands[-1], log_pivots(cands)


def solution(mesh):
    in_specs = (
        P(("band", "grid"), None),
        P(("band", "grid"), None),
        P(("band", "grid"), None),
        P("grid", None, None),
    )
    out_specs = (P(), P("grid", None))
    return jax.shard_map(local, mesh=mesh, in_specs=in_specs, out_specs=out_specs, check_vma=False)
```

```python
import functools

import jax
import jax.numpy as jnp
from jax import lax
from jax.experimental import pallas as pl
from jax.experimental.pallas import tpu as pltpu
from jax.sharding import PartitionSpec as P

ridge = 0.1
f32, bf16, f16 = jnp.float32, jnp.bfloat16, jnp.float16
step, height, lanes = 8, 32, 128
top, tag_rows = 14.0, 16
column_dims = (((0,), (0,)), ((), ()))


def bits_of(count):
    return count.bit_length() - 1


def exchange(block, axis, delta):
    count = lax.axis_size(axis)
    return lax.ppermute(block, axis, [(i, i ^ delta) for i in range(count)])


def reversed_bits(value, bits):
    out = 0
    for t in range(bits):
        out = out | ((value >> t) & 1) << (bits - 1 - t)
    return out


def pick(blocks, lists):
    out = []
    for block, listed in zip(blocks, lists):
        index = lax.broadcasted_iota(jnp.int32, (block.shape[1], listed.shape[0]), 0)
        one_hot = (index == listed).astype(bf16)
        out.append(jnp.dot(block, one_hot, preferred_element_type=f32).astype(bf16))
    return jnp.concatenate(out, axis=1)


def split3(v):
    a = v.astype(bf16)
    rest = v - a.astype(f32)
    b = rest.astype(bf16)
    c = (rest - b.astype(f32)).astype(bf16)
    return a, b, c


def eliminate(block, first):
    width = block.shape[1]
    lane = lax.broadcasted_iota(jnp.int32, (1, width), 1)
    on_diagonal = lax.broadcasted_iota(jnp.int32, (step, width), 1) - lax.broadcasted_iota(
        jnp.int32, (step, width), 0
    )
    done, scaled, diagonal = [], [], 0.0
    for corner in range(0, block.shape[0], step):
        below = lax.broadcasted_iota(jnp.int32, (block.shape[0], 1), 0)
        start = first + corner
        columns = [jnp.sum(jnp.where(lane == start + j, block, 0.0), axis=1, keepdims=True) for j in range(step)]
        heads, inverses = [], []
        for j in range(step):
            head = columns[j][j : j + 1, :]
            inverse = 1.0 / head
            factor = jnp.where(below > j, columns[j] * inverse, 0.0)
            block = block - factor * block[j : j + 1, :]
            for c in range(j + 1, step):
                columns[c] = columns[c] - factor * columns[c][j : j + 1, :]
            heads.append(head)
            inverses.append(inverse)
        heads = jnp.concatenate(heads, axis=0)
        diagonal = diagonal + jnp.sum(jnp.where(on_diagonal == start, heads, 0.0), axis=0, keepdims=True)
        done.append(block[:step])
        scaled.append(block[:step] * jnp.concatenate(inverses, axis=0))
        block = block[step:]
    return jnp.concatenate(done, axis=0), jnp.concatenate(scaled, axis=0), diagonal


def outer(scaled, rows):
    u1, u2, u3 = split3(rows)
    v1, v2, v3 = split3(scaled)
    left = jnp.concatenate([v1, v1, v2, v2, v1, v3], axis=0)
    right = jnp.concatenate([u1, u2, u1, u2, u3, u1], axis=0)
    return lax.dot_general(left, right, column_dims, preferred_element_type=f32)


def pivots_kernel(sets, *refs):
    cands, total_ref, out_ref, grams = refs[:sets], refs[sets], refs[sets + 1], refs[sets + 2 :]
    rows, n = cands[0].shape
    diagonal = lax.broadcasted_iota(jnp.int32, (n, n), 0) == lax.broadcasted_iota(jnp.int32, (n, n), 1)
    shift = jnp.where(diagonal, f32(ridge), f32(0))
    for cand, gram in zip(cands, grams):
        product = lax.dot_general(cand[...], cand[...], column_dims, preferred_element_type=f32)
        gram[...] = product * f32(1 / rows) + shift
    out_ref[...] = jnp.zeros_like(out_ref)
    for base in range(0, n, lanes):

        def panel(k, carry, base=base):
            first = pl.multiple_of(k * height, height)
            parts = [eliminate(gram[pl.ds(base + first, height), base:], first) for gram in grams]
            for q, (done, scaled, diagonal) in enumerate(parts):
                out_ref[q : q + 1, base:] += diagonal
                grams[q][base:, base:] -= outer(scaled, done)
            return carry

        lax.fori_loop(0, min(lanes, n - base) // height, panel, 0)
    total_ref[...] = jnp.sum(0.5 * jnp.log(out_ref[...]), axis=0, keepdims=True)


def log_pivots(cands):
    sets, (rows, n) = len(cands), cands[0].shape
    return pl.pallas_call(
        functools.partial(pivots_kernel, sets),
        out_shape=jax.ShapeDtypeStruct((1, n), f32),
        in_specs=[pl.BlockSpec(memory_space=pltpu.VMEM)] * sets,
        out_specs=pl.BlockSpec(memory_space=pltpu.VMEM),
        scratch_shapes=[pltpu.VMEM((sets, n), f32)] + [pltpu.VMEM((n, n), f32)] * sets,
        compiler_params=pltpu.CompilerParams(vmem_limit_bytes=40 << 20),
    )(*cands)


def half_of(block, upper):
    size = block.shape[-1] // 2
    return lax.dynamic_slice_in_dim(block, upper * size, size, axis=block.ndim - 1)


def sketch_kernel(mode, which, columns, starts, dots, plain, coded, *refs):
    refs, out_ref = refs[:-1], refs[-1]
    mixes, refs = refs[:dots], refs[dots:]
    views = [ref.at[:, start : start + columns] for ref, start in zip(refs, starts)]
    points, terms, codes = views[:dots], views[dots : dots + plain], views[dots + plain :]
    size = (out_ref.shape[0] - tag_rows) // len(which) if mode == "code" else out_ref.shape[0] // len(which)
    size = out_ref.shape[0] if mode == "multiply" else size
    totals = []
    for i in which:
        total = 0.0
        for mix_ref, points_ref in zip(mixes, points):
            total += lax.dot_general(mix_ref[i], points_ref[...], column_dims, preferred_element_type=f32)
        for term in terms:
            total += term[i * size : (i + 1) * size, :]
        first = 0
        for count in coded:
            code = codes[first + i] if count > 1 else codes[first]
            row = 0 if count > 1 else i * size
            last = code.shape[0] - tag_rows
            total += code[row : row + size, :] * jnp.exp2(code[last : last + 1, :] - top)
            first += count
        totals.append(total)
    if mode == "code":
        largest = functools.reduce(jnp.maximum, [jnp.max(jnp.abs(t), axis=(0, 1), keepdims=True) for t in totals])
        exponent = jnp.ceil(jnp.log2(jnp.maximum(largest, f32(1e-30))))
        for j, total in enumerate(totals):
            out_ref[j * size : (j + 1) * size, :] = total * jnp.exp2(top - exponent)
        out_ref[len(which) * size :, :] = jnp.broadcast_to(exponent, (tag_rows, columns))
    elif mode == "keep":
        for j, total in enumerate(totals):
            out_ref[j * size : (j + 1) * size, :] = total
    else:
        out_ref[...] = (totals[0] * totals[1]).astype(bf16)


def sketch(mode, which, block, mixes, plain=()):
    columns, points, coded = block
    size = mixes[0].shape[2]
    shapes = {"code": (len(which) * size + tag_rows, f32), "keep": (len(which) * size, f32), "multiply": (size, bf16)}
    rows, kind = shapes[mode]
    terms = list(points) + list(plain) + [term for item in coded for term in item]
    operands = list(mixes[: len(points)]) + [array for array, _ in terms]
    starts = [start for _, start in terms]
    counts = [len(item) for item in coded]
    return pl.pallas_call(
        functools.partial(sketch_kernel, mode, which, columns, starts, len(points), len(plain), counts),
        out_shape=jax.ShapeDtypeStruct((rows, columns), kind),
        in_specs=[pl.BlockSpec(memory_space=pltpu.VMEM)] * len(operands),
        out_specs=pl.BlockSpec(memory_space=pltpu.VMEM),
        compiler_params=pltpu.CompilerParams(vmem_limit_bytes=48 << 20),
    )(*operands)


def halves(block):
    columns, points, coded = block
    size = columns // 2
    return [
        [size, [(a, first + shift) for a, first in points], [[(a, first + shift) for a, first in c] for c in coded]]
        for shift in (0, size)
    ]


def local(orbitals, w_first, w_second, pivots):
    here, place = lax.axis_index("grid"), lax.axis_index("band")
    groups = lax.axis_size("grid")
    grid_bits, band_bits = bits_of(groups), bits_of(lax.axis_size("band"))
    order = pivots[0]
    kept = order.shape[1]
    width = orbitals.shape[1] // groups

    parts = 2 if grid_bits > 1 else 1
    count = groups // 2 // parts
    places = [[reversed_bits(p * count + i, grid_bits - 1) for i in range(count)] for p in range(parts)]

    def blocks_of(p, side):
        return [
            lax.dynamic_slice_in_dim(orbitals, (here ^ 2 * k + side) * width, width, axis=1) for k in places[p]
        ]

    raw = exchange(jnp.concatenate(blocks_of(parts - 1, 1), axis=1), "grid", 1)

    mixing = [jnp.stack([w_first, w_second])]
    for t in reversed(range(1, band_bits)):
        upper = place >> t & 1
        got = [exchange(half_of(m, 1 - upper), "band", 1 << t) for m in mixing]
        mixing = [half_of(m, upper) for m in mixing] + got
    near = mixing[0]

    orders = order[:1]
    for t in reversed(range(1, grid_bits)):
        if t == 1:
            orders, raw, near, mixing = lax.optimization_barrier((orders, raw, near, mixing))
        orders = jnp.stack([orders, exchange(orders, "grid", 1 << t)], axis=1).reshape(-1, kept)
    near = [near] + mixing[1:]
    near = [exchange(m, "grid", 1) for m in near]

    def over_bands(block):
        blocks = [block]
        for t in reversed(range(1, band_bits)):
            blocks = blocks + [exchange(m, "band", 1 << t) for m in blocks]
        return blocks

    def lists_of(p):
        return jnp.stack([orders[k] for k in places[p]])

    def gather(own, far):
        return jnp.concatenate(over_bands(own) + over_bands(far), axis=0)

    def over_cores(rows):
        return [(rows, 0), (exchange(rows, "band", 1), 0)]

    def swap(block, bit, sets):
        codes = [sketch("code", which, block, mixes).astype(f16) for which in sets]
        return [exchange(code, "grid", 1 << bit) for code in codes]

    picked = {}
    for p in reversed(range(parts)):
        listed = lists_of(p)
        own = pick(blocks_of(p, 0), listed)
        if p == parts - 1:
            far = pick([raw[:, i * width : (i + 1) * width] for i in range(count)], listed)
            orders, own, far = lax.optimization_barrier((orders, own, far))
        else:
            far = exchange(pick(blocks_of(p, 1), exchange(listed, "grid", 1)), "grid", 1)
        picked[p] = own, far

    both, each = [(0, 1)], [(0,), (1,)]
    go = [count * kept, over_cores(gather(*picked[parts - 1])), []]
    mixing = jnp.concatenate(mixing + near, axis=1)
    mixes = [half_of(mixing, place & 1), exchange(half_of(mixing, 1 - (place & 1)), "band", 1)]
    if parts > 1:
        stay = None
        for t in range(1, grid_bits):
            pieces = halves(go) if t < grid_bits - 1 else [go]
            coded = [swap(piece, t, each if piece is pieces[-1] else both) for piece in reversed(pieces)]
            if stay is None:
                rows = gather(*picked[0])
                coded[0], rows = lax.optimization_barrier((coded[0], rows))
                stay = [count * kept, over_cores(rows), []]
            got = [[(code.astype(f32), 0) for code in codes] for codes in reversed(coded)]
            if len(pieces) > 1:
                stay, go = [[n, points, codes + [new]] for (n, points, codes), new in zip(halves(stay), got)]
        held = sketch("keep", (0, 1), stay, mixes)
        chosen = sketch("multiply", (0, 1), [kept, [], got], mixes, [(held, 0)])
    else:
        chosen = sketch("multiply", (0, 1), go, mixes)

    def over_band(block):
        for t in reversed(range(band_bits)):
            got = exchange(block, "band", 1 << t)
            upper = place >> t & 1 == 1
            count = 1 << (band_bits - 1 - t)
            share = block.reshape((count, -1) + block.shape[1:])
            other = got.reshape(share.shape)
            low, high = jnp.where(upper, other, share), jnp.where(upper, share, other)
            block = jnp.concatenate([low, high], axis=1).reshape((-1,) + block.shape[1:])
        return block

    cands = [over_band(chosen)]
    index = lax.broadcasted_iota(jnp.int32, (kept, kept), 0)
    for section in range(1, grid_bits + 1):
        got = exchange(chosen, "grid", 1 << section - 1)
        upper = here >> section - 1 & 1
        mine = (index == order[section] - upper * kept).astype(bf16)
        other = (index == order[section] - (1 - upper) * kept).astype(bf16)
        chosen = jnp.dot(chosen, mine, preferred_element_type=f32) + jnp.dot(got, other, preferred_element_type=f32)
        chosen = chosen.astype(bf16)
        cands.append(over_band(chosen))
    return cands[-1], log_pivots(cands)


def solution(mesh):
    in_specs = (
        P(("band", "grid"), None),
        P(("band", "grid"), None),
        P(("band", "grid"), None),
        P("grid", None, None),
    )
    out_specs = (P(), P("grid", None))
    return jax.shard_map(local, mesh=mesh, in_specs=in_specs, out_specs=out_specs, check_vma=False)
```

```python
import functools

import jax
import jax.numpy as jnp
from jax import lax
from jax.experimental import pallas as pl
from jax.experimental.pallas import tpu as pltpu
from jax.sharding import PartitionSpec as P

ridge = 0.1
f32, bf16, f16 = jnp.float32, jnp.bfloat16, jnp.float16
step, height, lanes = 8, 32, 128
top, tag_rows = 14.0, 16
column_dims = (((0,), (0,)), ((), ()))


def bits_of(count):
    return count.bit_length() - 1


def exchange(block, axis, delta):
    count = lax.axis_size(axis)
    return lax.ppermute(block, axis, [(i, i ^ delta) for i in range(count)])


def reversed_bits(value, bits):
    out = 0
    for t in range(bits):
        out = out | ((value >> t) & 1) << (bits - 1 - t)
    return out


def pick(blocks, lists):
    out = []
    for block, listed in zip(blocks, lists):
        index = lax.broadcasted_iota(jnp.int32, (block.shape[1], listed.shape[0]), 0)
        one_hot = (index == listed).astype(bf16)
        out.append(jnp.dot(block, one_hot, preferred_element_type=f32).astype(bf16))
    return jnp.concatenate(out, axis=1)


def split3(v):
    a = v.astype(bf16)
    rest = v - a.astype(f32)
    b = rest.astype(bf16)
    c = (rest - b.astype(f32)).astype(bf16)
    return a, b, c


def eliminate(block, first):
    width = block.shape[1]
    lane = lax.broadcasted_iota(jnp.int32, (1, width), 1)
    on_diagonal = lax.broadcasted_iota(jnp.int32, (step, width), 1) - lax.broadcasted_iota(
        jnp.int32, (step, width), 0
    )
    done, scaled, diagonal = [], [], 0.0
    for corner in range(0, block.shape[0], step):
        below = lax.broadcasted_iota(jnp.int32, (block.shape[0], 1), 0)
        start = first + corner
        columns = [jnp.sum(jnp.where(lane == start + j, block, 0.0), axis=1, keepdims=True) for j in range(step)]
        heads, inverses = [], []
        for j in range(step):
            head = columns[j][j : j + 1, :]
            inverse = 1.0 / head
            factor = jnp.where(below > j, columns[j] * inverse, 0.0)
            block = block - factor * block[j : j + 1, :]
            for c in range(j + 1, step):
                columns[c] = columns[c] - factor * columns[c][j : j + 1, :]
            heads.append(head)
            inverses.append(inverse)
        heads = jnp.concatenate(heads, axis=0)
        diagonal = diagonal + jnp.sum(jnp.where(on_diagonal == start, heads, 0.0), axis=0, keepdims=True)
        done.append(block[:step])
        scaled.append(block[:step] * jnp.concatenate(inverses, axis=0))
        block = block[step:]
    return jnp.concatenate(done, axis=0), jnp.concatenate(scaled, axis=0), diagonal


def outer(scaled, rows):
    u1, u2, u3 = split3(rows)
    v1, v2, v3 = split3(scaled)
    left = jnp.concatenate([v1, v1, v2, v2, v1, v3], axis=0)
    right = jnp.concatenate([u1, u2, u1, u2, u3, u1], axis=0)
    return lax.dot_general(left, right, column_dims, preferred_element_type=f32)


def pivots_kernel(sets, late, *refs):
    grams, refs = refs[:sets], refs[sets:]
    if late:
        place_ref, cand_ref, refs = refs[0], refs[1], refs[2:]
    total_ref, work, diagonals = refs[0], refs[1:-1], refs[-1]
    n = grams[0].shape[0]
    for gram, matrix in zip(grams, work):
        matrix[...] = gram[...]
    if late:
        product = lax.dot_general(cand_ref[...], cand_ref[...], column_dims, preferred_element_type=f32)
        last = work[-1]
        last[...] = jnp.where(place_ref[0] & 1 == 0, last[...], shifted(product, cand_ref.shape[0]))
    diagonals[...] = jnp.zeros_like(diagonals)
    for base in range(0, n, lanes):

        def panel(k, carry, base=base):
            first = pl.multiple_of(k * height, height)
            parts = [eliminate(matrix[pl.ds(base + first, height), base:], first) for matrix in work]
            for q, (done, scaled, diagonal) in enumerate(parts):
                diagonals[q : q + 1, base:] += diagonal
                work[q][base:, base:] -= outer(scaled, done)
            return carry

        lax.fori_loop(0, min(lanes, n - base) // height, panel, 0)
    total_ref[...] = jnp.sum(0.5 * jnp.log(diagonals[...]), axis=0, keepdims=True)


def shifted(product, rows):
    n = product.shape[0]
    diagonal = lax.broadcasted_iota(jnp.int32, (n, n), 0) == lax.broadcasted_iota(jnp.int32, (n, n), 1)
    return product * f32(1 / rows) + jnp.where(diagonal, f32(ridge), f32(0))


def gram_of(blocks):
    product = sum(lax.dot_general(b, b, column_dims, preferred_element_type=f32) for b in blocks)
    return shifted(product, sum(b.shape[0] for b in blocks))


def log_pivots(grams, place=None, cand=None):
    sets, n = len(grams), grams[0].shape[0]
    operands, specs = list(grams), [pl.BlockSpec(memory_space=pltpu.VMEM)] * sets
    if cand is not None:
        operands += [place[None], cand]
        specs += [pl.BlockSpec(memory_space=pltpu.SMEM), pl.BlockSpec(memory_space=pltpu.VMEM)]
    return pl.pallas_call(
        functools.partial(pivots_kernel, sets, cand is not None),
        out_shape=jax.ShapeDtypeStruct((1, n), f32),
        in_specs=specs,
        out_specs=pl.BlockSpec(memory_space=pltpu.VMEM),
        scratch_shapes=[pltpu.VMEM((n, n), f32)] * sets + [pltpu.VMEM((sets, n), f32)],
        compiler_params=pltpu.CompilerParams(vmem_limit_bytes=40 << 20),
    )(*operands)


def half_of(block, upper):
    size = block.shape[-1] // 2
    return lax.dynamic_slice_in_dim(block, upper * size, size, axis=block.ndim - 1)


def sketch_kernel(mode, columns, starts, dots, plain, *refs):
    refs, out_ref = refs[:-1], refs[-1]
    mixes, refs = refs[:dots], refs[dots:]
    views = [ref.at[:, start : start + columns] for ref, start in zip(refs, starts)]
    points, terms, coded = views[:dots], views[dots : dots + plain], views[dots + plain :]
    size = {"code": out_ref.shape[0] - tag_rows, "keep": out_ref.shape[0], "multiply": 2 * out_ref.shape[0]}[mode] // 2
    totals = []
    for i in range(2):
        own, total = pl.ds(i * size, size), 0.0
        for mix_ref, points_ref in zip(mixes, points):
            total += lax.dot_general(mix_ref[i], points_ref[...], column_dims, preferred_element_type=f32)
        for term in terms:
            total += term[own, :]
        for codes in coded:
            total += codes[own, :] * jnp.exp2(codes[2 * size : 2 * size + 1, :] - top)
        totals.append(total)
    if mode == "code":
        largest = jnp.maximum(*[jnp.max(jnp.abs(t), axis=(0, 1), keepdims=True) for t in totals])
        exponent = jnp.ceil(jnp.log2(jnp.maximum(largest, f32(1e-30))))
        totals = [total * jnp.exp2(top - exponent) for total in totals]
        out_ref[2 * size :, :] = jnp.broadcast_to(exponent, (tag_rows, columns))
    if mode == "multiply":
        out_ref[...] = (totals[0] * totals[1]).astype(bf16)
    else:
        for i in range(2):
            out_ref[i * size : (i + 1) * size, :] = totals[i]


def sketch(mode, block, mixes, plain=()):
    columns, points, coded = block
    size = mixes[0].shape[2]
    rows, kind = {"code": (2 * size + tag_rows, f32), "keep": (2 * size, f32), "multiply": (size, bf16)}[mode]
    terms = list(points) + list(plain) + list(coded)
    operands = list(mixes[: len(points)]) + [array for array, _ in terms]
    return pl.pallas_call(
        functools.partial(sketch_kernel, mode, columns, [start for _, start in terms], len(points), len(plain)),
        out_shape=jax.ShapeDtypeStruct((rows, columns), kind),
        in_specs=[pl.BlockSpec(memory_space=pltpu.VMEM)] * len(operands),
        out_specs=pl.BlockSpec(memory_space=pltpu.VMEM),
        compiler_params=pltpu.CompilerParams(vmem_limit_bytes=48 << 20),
    )(*operands)


def halves(block):
    size = block[0] // 2
    return [[size] + [[(a, first + shift) for a, first in terms] for terms in block[1:]] for shift in (0, size)]


def local(orbitals, w_first, w_second, pivots):
    here, place = lax.axis_index("grid"), lax.axis_index("band")
    groups = lax.axis_size("grid")
    grid_bits, band_bits = bits_of(groups), bits_of(lax.axis_size("band"))
    order = pivots[0]
    kept = order.shape[1]
    width = orbitals.shape[1] // groups

    parts = 2 if grid_bits > 1 else 1
    count = groups // 2 // parts
    places = [[reversed_bits(p * count + i, grid_bits - 1) for i in range(count)] for p in range(parts)]

    def blocks_of(p, side):
        return [
            lax.dynamic_slice_in_dim(orbitals, (here ^ 2 * k + side) * width, width, axis=1) for k in places[p]
        ]

    raw = exchange(jnp.concatenate(blocks_of(parts - 1, 1), axis=1), "grid", 1)

    mixing = [jnp.stack([w_first, w_second])]
    for t in reversed(range(1, band_bits)):
        upper = place >> t & 1
        got = [exchange(half_of(m, 1 - upper), "band", 1 << t) for m in mixing]
        mixing = [half_of(m, upper) for m in mixing] + got
    near = mixing[0]

    orders = order[:1]
    for t in reversed(range(2, grid_bits)):
        orders = jnp.stack([orders, exchange(orders, "grid", 1 << t)], axis=1).reshape(-1, kept)
    if parts > 1:
        listed = jnp.concatenate([orders[k >> 1] for k in places[0]])
        size, span = near.shape[1:]
        digits = jnp.stack([listed >> 8, listed & 255]).astype(bf16)
        digits = jnp.pad(digits, ((0, 0), (0, -listed.shape[0] % (16 * span)))).reshape(2, -1, span)
        near = exchange(jnp.concatenate([near, digits], axis=1), "grid", 1)
        near, digits = near[:, :size], near[:, size:].reshape(2, -1)[:, : listed.shape[0]].astype(jnp.int32)
        far_lists = (digits[0] * 256 + digits[1]).reshape(-1, kept)
        orders = jnp.stack([orders, exchange(orders, "grid", 2)], axis=1).reshape(-1, kept)
    else:
        near = exchange(near, "grid", 1)
    near = [near] + [exchange(m, "grid", 1) for m in mixing[1:]]

    def over_bands(block):
        blocks = [block]
        for t in reversed(range(1, band_bits)):
            blocks = blocks + [exchange(m, "band", 1 << t) for m in blocks]
        return blocks

    def lists_of(p):
        return [orders[k] for k in places[p]]

    def gather(own, far):
        return jnp.concatenate(over_bands(own) + over_bands(far), axis=0)

    def over_cores(rows):
        return [(rows, 0), (exchange(rows, "band", 1), 0)]

    picked = {}
    for p in reversed(range(parts)):
        own = pick(blocks_of(p, 0), lists_of(p))
        if p == parts - 1:
            far = pick([raw[:, i * width : (i + 1) * width] for i in range(count)], lists_of(p))
            if parts > 1:
                orders, far_lists, _, _ = lax.optimization_barrier((orders, far_lists, own, far))
        else:
            far = exchange(pick(blocks_of(p, 1), far_lists), "grid", 1)
        picked[p] = own, far

    go = [count * kept, over_cores(gather(*picked[parts - 1])), []]
    mixing = jnp.concatenate(mixing + near, axis=1)
    mixes = [half_of(mixing, place & 1), exchange(half_of(mixing, 1 - (place & 1)), "band", 1)]

    def swap(block, bit):
        return exchange(sketch("code", block, mixes).astype(f16), "grid", 1 << bit)

    if parts > 1:
        stay = None
        for t in range(1, grid_bits):
            pieces = halves(go) if t < grid_bits - 1 else [go]
            got = [swap(piece, t) for piece in reversed(pieces)]
            if stay is None:
                got[0], rows = lax.optimization_barrier((got[0], gather(*picked[0])))
                stay = [count * kept, over_cores(rows), []]
            if len(pieces) > 1:
                stay, go = halves(stay)
                for block, codes in zip((go, stay), got):
                    block[2].append((codes.astype(f32), 0))
        held = sketch("keep", stay, mixes)
        chosen = sketch("multiply", [kept, [], [(got[0].astype(f32), 0)]], mixes, [(held, 0)])
    else:
        chosen = sketch("multiply", go, mixes)

    def in_order(block, got, t):
        upper = place >> t & 1 == 1
        count = 1 << (band_bits - 1 - t)
        share = block.reshape((count, -1) + block.shape[1:])
        other = got.reshape(share.shape)
        low, high = jnp.where(upper, other, share), jnp.where(upper, share, other)
        return jnp.concatenate([low, high], axis=1).reshape((-1,) + block.shape[1:])

    def over_higher(block):
        for t in reversed(range(1, band_bits)):
            block = in_order(block, exchange(block, "band", 1 << t), t)
        return block

    rounds = grid_bits + 1
    paired = rounds - 2 + rounds % 2
    index = lax.broadcasted_iota(jnp.int32, (kept, kept), 0)
    even = place & 1 == 0
    shared, grams = [], []
    for section in range(rounds):
        if section:
            got = exchange(chosen, "grid", 1 << section - 1)
            upper = here >> section - 1 & 1
            mine = (index == order[section] - upper * kept).astype(bf16)
            other = (index == order[section] - (1 - upper) * kept).astype(bf16)
            chosen = jnp.dot(chosen, mine, preferred_element_type=f32) + jnp.dot(got, other, preferred_element_type=f32)
            chosen = chosen.astype(bf16)
        if section == rounds - 1:
            final = over_higher(chosen)
        else:
            block = chosen
            if shared:
                block, shared[-1] = lax.optimization_barrier((block, shared[-1]))
            shared.append(over_higher(block))
            if section < paired and section % 2:
                low, high = shared[-2:]
                got = exchange(jnp.where(even, high, low), "band", 1)
                grams.append(gram_of([jnp.where(even, low, high), got]))
    cands = in_order(final, exchange(final, "band", 1), 0)
    if rounds % 2:
        odd = log_pivots([gram_of([cands])])
        quality = jnp.where(even, 0.0, odd) + (log_pivots(grams) if grams else 0.0)
    else:
        last = gram_of([shared[-1], exchange(shared[-1], "band", 1)])
        quality = log_pivots(grams + [last], place, cands)
    return cands, quality + exchange(quality, "band", 1)


def solution(mesh):
    in_specs = (
        P(("band", "grid"), None),
        P(("band", "grid"), None),
        P(("band", "grid"), None),
        P("grid", None, None),
    )
    out_specs = (P(), P("grid", None))
    return jax.shard_map(local, mesh=mesh, in_specs=in_specs, out_specs=out_specs, check_vma=False)
```

```python
import functools

import jax
import jax.numpy as jnp
from jax import lax
from jax.experimental import pallas as pl
from jax.experimental.pallas import tpu as pltpu
from jax.sharding import PartitionSpec as P

ridge = 0.1
f32, bf16, f16 = jnp.float32, jnp.bfloat16, jnp.float16
step, height, lanes = 8, 32, 128
top, tag_rows = 14.0, 16
column_dims = (((0,), (0,)), ((), ()))


def bits_of(count):
    return count.bit_length() - 1


def exchange(block, axis, delta):
    count = lax.axis_size(axis)
    return lax.ppermute(block, axis, [(i, i ^ delta) for i in range(count)])


def reversed_bits(value, bits):
    out = 0
    for t in range(bits):
        out = out | ((value >> t) & 1) << (bits - 1 - t)
    return out


def pick(blocks, lists):
    out = []
    for block, listed in zip(blocks, lists):
        index = lax.broadcasted_iota(jnp.int32, (block.shape[1], listed.shape[0]), 0)
        one_hot = (index == listed).astype(bf16)
        out.append(jnp.dot(block, one_hot, preferred_element_type=f32).astype(bf16))
    return jnp.concatenate(out, axis=1)


def split3(v):
    a = v.astype(bf16)
    rest = v - a.astype(f32)
    b = rest.astype(bf16)
    c = (rest - b.astype(f32)).astype(bf16)
    return a, b, c


def eliminate(block, first):
    width = block.shape[1]
    lane = lax.broadcasted_iota(jnp.int32, (1, width), 1)
    on_diagonal = lax.broadcasted_iota(jnp.int32, (step, width), 1) - lax.broadcasted_iota(
        jnp.int32, (step, width), 0
    )
    done, scaled, diagonal = [], [], 0.0
    for corner in range(0, block.shape[0], step):
        below = lax.broadcasted_iota(jnp.int32, (block.shape[0], 1), 0)
        start = first + corner
        columns = [jnp.sum(jnp.where(lane == start + j, block, 0.0), axis=1, keepdims=True) for j in range(step)]
        heads, inverses = [], []
        for j in range(step):
            head = columns[j][j : j + 1, :]
            inverse = 1.0 / head
            factor = jnp.where(below > j, columns[j] * inverse, 0.0)
            block = block - factor * block[j : j + 1, :]
            for c in range(j + 1, step):
                columns[c] = columns[c] - factor * columns[c][j : j + 1, :]
            heads.append(head)
            inverses.append(inverse)
        heads = jnp.concatenate(heads, axis=0)
        diagonal = diagonal + jnp.sum(jnp.where(on_diagonal == start, heads, 0.0), axis=0, keepdims=True)
        done.append(block[:step])
        scaled.append(block[:step] * jnp.concatenate(inverses, axis=0))
        block = block[step:]
    return jnp.concatenate(done, axis=0), jnp.concatenate(scaled, axis=0), diagonal


def outer(scaled, rows):
    u1, u2, u3 = split3(rows)
    v1, v2, v3 = split3(scaled)
    left = jnp.concatenate([v1, v1, v2, v2, v1, v3], axis=0)
    right = jnp.concatenate([u1, u2, u1, u2, u3, u1], axis=0)
    return lax.dot_general(left, right, column_dims, preferred_element_type=f32)


def pivots_kernel(sets, late, *refs):
    grams, refs = refs[:sets], refs[sets:]
    if late:
        place_ref, cand_ref, refs = refs[0], refs[1], refs[2:]
    total_ref, work, diagonals = refs[0], refs[1:-1], refs[-1]
    n = grams[0].shape[0]
    for gram, matrix in zip(grams, work):
        matrix[...] = gram[...]
    if late:
        product = lax.dot_general(cand_ref[...], cand_ref[...], column_dims, preferred_element_type=f32)
        last = work[-1]
        last[...] = jnp.where(place_ref[0] & 1 == 0, last[...], shifted(product, cand_ref.shape[0]))
    diagonals[...] = jnp.zeros_like(diagonals)
    for base in range(0, n, lanes):

        def panel(k, carry, base=base):
            first = pl.multiple_of(k * height, height)
            parts = [eliminate(matrix[pl.ds(base + first, height), base:], first) for matrix in work]
            for q, (done, scaled, diagonal) in enumerate(parts):
                diagonals[q : q + 1, base:] += diagonal
                work[q][base:, base:] -= outer(scaled, done)
            return carry

        lax.fori_loop(0, min(lanes, n - base) // height, panel, 0)
    total_ref[...] = jnp.sum(0.5 * jnp.log(diagonals[...]), axis=0, keepdims=True)


def shifted(product, rows):
    n = product.shape[0]
    diagonal = lax.broadcasted_iota(jnp.int32, (n, n), 0) == lax.broadcasted_iota(jnp.int32, (n, n), 1)
    return product * f32(1 / rows) + jnp.where(diagonal, f32(ridge), f32(0))


def gram_of(blocks):
    product = sum(lax.dot_general(b, b, column_dims, preferred_element_type=f32) for b in blocks)
    return shifted(product, sum(b.shape[0] for b in blocks))


def log_pivots(grams, place=None, cand=None):
    sets, n = len(grams), grams[0].shape[0]
    operands, specs = list(grams), [pl.BlockSpec(memory_space=pltpu.VMEM)] * sets
    if cand is not None:
        operands += [place[None], cand]
        specs += [pl.BlockSpec(memory_space=pltpu.SMEM), pl.BlockSpec(memory_space=pltpu.VMEM)]
    return pl.pallas_call(
        functools.partial(pivots_kernel, sets, cand is not None),
        out_shape=jax.ShapeDtypeStruct((1, n), f32),
        in_specs=specs,
        out_specs=pl.BlockSpec(memory_space=pltpu.VMEM),
        scratch_shapes=[pltpu.VMEM((n, n), f32)] * sets + [pltpu.VMEM((sets, n), f32)],
        compiler_params=pltpu.CompilerParams(vmem_limit_bytes=40 << 20),
    )(*operands)


def half_of(block, upper):
    size = block.shape[-1] // 2
    return lax.dynamic_slice_in_dim(block, upper * size, size, axis=block.ndim - 1)


def sketch_kernel(mode, columns, starts, dots, plain, *refs):
    refs, out_ref = refs[:-1], refs[-1]
    mixes, refs = refs[:dots], refs[dots:]
    views = [ref.at[:, start : start + columns] for ref, start in zip(refs, starts)]
    points, terms, coded = views[:dots], views[dots : dots + plain], views[dots + plain :]
    size = {"code": out_ref.shape[0] - tag_rows, "keep": out_ref.shape[0], "multiply": 2 * out_ref.shape[0]}[mode] // 2
    totals = []
    for i in range(2):
        own, total = pl.ds(i * size, size), 0.0
        for mix_ref, points_ref in zip(mixes, points):
            total += lax.dot_general(mix_ref[i], points_ref[...], column_dims, preferred_element_type=f32)
        for term in terms:
            total += term[own, :]
        for codes in coded:
            total += codes[own, :] * jnp.exp2(codes[2 * size : 2 * size + 1, :] - top)
        totals.append(total)
    if mode == "code":
        largest = jnp.maximum(*[jnp.max(jnp.abs(t), axis=(0, 1), keepdims=True) for t in totals])
        exponent = jnp.ceil(jnp.log2(jnp.maximum(largest, f32(1e-30))))
        totals = [total * jnp.exp2(top - exponent) for total in totals]
        out_ref[2 * size :, :] = jnp.broadcast_to(exponent, (tag_rows, columns))
    if mode == "multiply":
        out_ref[...] = (totals[0] * totals[1]).astype(bf16)
    else:
        for i in range(2):
            out_ref[i * size : (i + 1) * size, :] = totals[i]


def sketch(mode, block, mixes, plain=()):
    columns, points, coded = block
    size = mixes[0].shape[2]
    rows, kind = {"code": (2 * size + tag_rows, f32), "keep": (2 * size, f32), "multiply": (size, bf16)}[mode]
    terms = list(points) + list(plain) + list(coded)
    operands = list(mixes[: len(points)]) + [array for array, _ in terms]
    return pl.pallas_call(
        functools.partial(sketch_kernel, mode, columns, [start for _, start in terms], len(points), len(plain)),
        out_shape=jax.ShapeDtypeStruct((rows, columns), kind),
        in_specs=[pl.BlockSpec(memory_space=pltpu.VMEM)] * len(operands),
        out_specs=pl.BlockSpec(memory_space=pltpu.VMEM),
        compiler_params=pltpu.CompilerParams(vmem_limit_bytes=48 << 20),
    )(*operands)


def halves(block):
    size = block[0] // 2
    return [[size] + [[(a, first + shift) for a, first in terms] for terms in block[1:]] for shift in (0, size)]


def local(orbitals, w_first, w_second, pivots):
    here, place = lax.axis_index("grid"), lax.axis_index("band")
    groups = lax.axis_size("grid")
    grid_bits, band_bits = bits_of(groups), bits_of(lax.axis_size("band"))
    order = pivots[0]
    kept = order.shape[1]
    width = orbitals.shape[1] // groups

    parts = 2 if grid_bits > 1 else 1
    count = groups // 2 // parts
    places = [[reversed_bits(p * count + i, grid_bits - 1) for i in range(count)] for p in range(parts)]

    def blocks_of(p, side):
        return [
            lax.dynamic_slice_in_dim(orbitals, (here ^ 2 * k + side) * width, width, axis=1) for k in places[p]
        ]

    raw = exchange(jnp.concatenate(blocks_of(parts - 1, 1), axis=1), "grid", 1)

    mixing = [jnp.stack([w_first, w_second])]
    for t in reversed(range(1, band_bits)):
        upper = place >> t & 1
        got = [exchange(half_of(m, 1 - upper), "band", 1 << t) for m in mixing]
        mixing = [half_of(m, upper) for m in mixing] + got
    near = mixing[0]

    orders = order[:1]
    for t in reversed(range(2, grid_bits)):
        orders = jnp.stack([orders, exchange(orders, "grid", 1 << t)], axis=1).reshape(-1, kept)
    if parts > 1:
        listed = jnp.concatenate([orders[k >> 1] for k in places[0]])
        size, span = near.shape[1:]
        digits = jnp.stack([listed >> 8, listed & 255]).astype(bf16)
        digits = jnp.pad(digits, ((0, 0), (0, -listed.shape[0] % (16 * span)))).reshape(2, -1, span)
        near = exchange(jnp.concatenate([near, digits], axis=1), "grid", 1)
        near, digits = near[:, :size], near[:, size:].reshape(2, -1)[:, : listed.shape[0]].astype(jnp.int32)
        far_lists = (digits[0] * 256 + digits[1]).reshape(-1, kept)
        orders = jnp.stack([orders, exchange(orders, "grid", 2)], axis=1).reshape(-1, kept)
    else:
        near = exchange(near, "grid", 1)
    near = [near] + [exchange(m, "grid", 1) for m in mixing[1:]]

    def over_bands(block):
        blocks = [block]
        for t in reversed(range(1, band_bits)):
            blocks = blocks + [exchange(m, "band", 1 << t) for m in blocks]
        return blocks

    def joined(rows):
        return jnp.concatenate(over_bands(rows), axis=0)

    def over_cores(rows):
        return [rows, exchange(rows, "band", 1)]

    def shares(matrices):
        whole = jnp.concatenate(matrices, axis=1)
        return [half_of(whole, place & 1), exchange(half_of(whole, 1 - (place & 1)), "band", 1)]

    own = pick([block for p in range(parts) for block in blocks_of(p, 0)], [orders[k] for p in places for k in p])
    far = [None] * parts
    far[-1] = pick([raw[:, i * width : (i + 1) * width] for i in range(count)], [orders[k] for k in places[-1]])
    if parts > 1:
        far[0] = exchange(pick(blocks_of(0, 1), far_lists), "grid", 1)
    own = over_cores(joined(own))
    mixes = shares(mixing) + shares(near)

    def block_of(p, rows):
        columns = count * kept
        return [columns, [(array, p * columns) for array in own] + [(array, 0) for array in over_cores(rows)], []]

    go = block_of(parts - 1, joined(far[-1]))

    if parts > 1:
        stay = None
        for t in range(1, grid_bits):
            pieces = halves(go) if t < grid_bits - 1 else [go]
            codes = [sketch("code", piece, mixes).astype(f16) for piece in reversed(pieces)]
            got = exchange(codes[0], "grid", 1 << t)
            if stay is None:
                codes[1:], rows = lax.optimization_barrier((codes[1:], far[0]))
                got, rows = lax.optimization_barrier((got, joined(rows)))
                stay = block_of(0, rows)
            if len(pieces) > 1:
                stay, go = halves(stay)
                go[2].append((got.astype(f32), 0))
                stay[2].append((exchange(codes[1], "grid", 1 << t).astype(f32), 0))
        held = sketch("keep", stay, mixes)
        chosen = sketch("multiply", [kept, [], [(got.astype(f32), 0)]], mixes, [(held, 0)])
    else:
        chosen = sketch("multiply", go, mixes)

    def in_order(block, got, t):
        upper = place >> t & 1 == 1
        count = 1 << (band_bits - 1 - t)
        share = block.reshape((count, -1) + block.shape[1:])
        other = got.reshape(share.shape)
        low, high = jnp.where(upper, other, share), jnp.where(upper, share, other)
        return jnp.concatenate([low, high], axis=1).reshape((-1,) + block.shape[1:])

    def over_higher(block):
        for t in reversed(range(1, band_bits)):
            block = in_order(block, exchange(block, "band", 1 << t), t)
        return block

    rounds = grid_bits + 1
    paired = rounds - 2 + rounds % 2
    index = lax.broadcasted_iota(jnp.int32, (kept, kept), 0)
    even = place & 1 == 0
    shared, grams = [], []
    for section in range(rounds):
        if section:
            got = exchange(chosen, "grid", 1 << section - 1)
            upper = here >> section - 1 & 1
            mine = (index == order[section] - upper * kept).astype(bf16)
            other = (index == order[section] - (1 - upper) * kept).astype(bf16)
            chosen = jnp.dot(chosen, mine, preferred_element_type=f32) + jnp.dot(got, other, preferred_element_type=f32)
            chosen = chosen.astype(bf16)
        if section == rounds - 1:
            final = over_higher(chosen)
        else:
            block = chosen
            if shared:
                block, shared[-1] = lax.optimization_barrier((block, shared[-1]))
            shared.append(over_higher(block))
            if section < paired and section % 2:
                low, high = shared[-2:]
                got = exchange(jnp.where(even, high, low), "band", 1)
                grams.append(gram_of([jnp.where(even, low, high), got]))
    cands = in_order(final, exchange(final, "band", 1), 0)
    if rounds % 2:
        odd = log_pivots([gram_of([cands])])
        quality = jnp.where(even, 0.0, odd) + (log_pivots(grams) if grams else 0.0)
    else:
        last = gram_of([shared[-1], exchange(shared[-1], "band", 1)])
        quality = log_pivots(grams + [last], place, cands)
    return cands, quality + exchange(quality, "band", 1)


def solution(mesh):
    in_specs = (
        P(("band", "grid"), None),
        P(("band", "grid"), None),
        P(("band", "grid"), None),
        P("grid", None, None),
    )
    out_specs = (P(), P("grid", None))
    return jax.shard_map(local, mesh=mesh, in_specs=in_specs, out_specs=out_specs, check_vma=False)
```

```python
import functools

import jax
import jax.numpy as jnp
from jax import lax
from jax.experimental import pallas as pl
from jax.experimental.pallas import tpu as pltpu
from jax.sharding import PartitionSpec as P

ridge = 0.1
f32, bf16, f16 = jnp.float32, jnp.bfloat16, jnp.float16
step, height, lanes = 8, 32, 128
top, tag_rows = 14.0, 16
column_dims = (((0,), (0,)), ((), ()))


def bits_of(count):
    return count.bit_length() - 1


def exchange(block, axis, delta):
    count = lax.axis_size(axis)
    return lax.ppermute(block, axis, [(i, i ^ delta) for i in range(count)])


def reversed_bits(value, bits):
    out = 0
    for t in range(bits):
        out = out | ((value >> t) & 1) << (bits - 1 - t)
    return out


def pick(blocks, lists):
    out = []
    for block, listed in zip(blocks, lists):
        index = lax.broadcasted_iota(jnp.int32, (block.shape[1], listed.shape[0]), 0)
        one_hot = (index == listed).astype(bf16)
        out.append(jnp.dot(block, one_hot, preferred_element_type=f32).astype(bf16))
    return jnp.concatenate(out, axis=1)


def split3(v):
    a = v.astype(bf16)
    rest = v - a.astype(f32)
    b = rest.astype(bf16)
    c = (rest - b.astype(f32)).astype(bf16)
    return a, b, c


def eliminate(block, first):
    width = min(lanes, block.shape[1])
    lane = lax.broadcasted_iota(jnp.int32, (1, width), 1)
    on_diagonal = lax.broadcasted_iota(jnp.int32, (step, width), 1) - lax.broadcasted_iota(
        jnp.int32, (step, width), 0
    )
    done, scaled, diagonal = [], [], 0.0
    for corner in range(0, block.shape[0], step):
        below = lax.broadcasted_iota(jnp.int32, (block.shape[0], 1), 0)
        start = first + corner
        near = block[:, :width]
        columns = [jnp.sum(jnp.where(lane == start + j, near, 0.0), axis=1, keepdims=True) for j in range(step)]
        heads, inverses = [], []
        for j in range(step):
            head = columns[j][j : j + 1, :]
            inverse = 1.0 / head
            factor = jnp.where(below > j, columns[j] * inverse, 0.0)
            block = block - factor * block[j : j + 1, :]
            for c in range(j + 1, step):
                columns[c] = columns[c] - factor * columns[c][j : j + 1, :]
            heads.append(head)
            inverses.append(inverse)
        heads = jnp.concatenate(heads, axis=0)
        diagonal = diagonal + jnp.sum(jnp.where(on_diagonal == start, heads, 0.0), axis=0, keepdims=True)
        done.append(block[:step])
        scaled.append(block[:step] * jnp.concatenate(inverses, axis=0))
        block = block[step:]
    return jnp.concatenate(done, axis=0), jnp.concatenate(scaled, axis=0), diagonal


def outer(scaled, rows):
    u1, u2, u3 = split3(rows)
    v1, v2, v3 = split3(scaled)
    left = jnp.concatenate([v1, v1, v2, v2, v1, v3], axis=0)
    right = jnp.concatenate([u1, u2, u1, u2, u3, u1], axis=0)
    return lax.dot_general(left, right, column_dims, preferred_element_type=f32)


def pivots_kernel(sets, late, *refs):
    grams, refs = refs[:sets], refs[sets:]
    if late:
        place_ref, cand_ref, refs = refs[0], refs[1], refs[2:]
    total_ref, work, diagonals = refs[0], refs[1:-1], refs[-1]
    n = grams[0].shape[0]
    for gram, matrix in zip(grams, work):
        matrix[...] = gram[...]
    if late:
        product = lax.dot_general(cand_ref[...], cand_ref[...], column_dims, preferred_element_type=f32)
        last = work[-1]
        last[...] = jnp.where(place_ref[0] & 1 == 0, last[...], shifted(product, cand_ref.shape[0]))
    diagonals[...] = jnp.zeros_like(diagonals)
    for base in range(0, n, lanes):

        def panel(k, carry, base=base):
            first = pl.multiple_of(k * height, height)
            parts = [eliminate(matrix[pl.ds(base + first, height), base:], first) for matrix in work]
            for q, (done, scaled, diagonal) in enumerate(parts):
                diagonals[q : q + 1, base : base + diagonal.shape[1]] += diagonal
                work[q][base:, base:] -= outer(scaled, done)
            return carry

        lax.fori_loop(0, min(lanes, n - base) // height, panel, 0)
    total_ref[...] = jnp.sum(0.5 * jnp.log(diagonals[...]), axis=0, keepdims=True)


def shifted(product, rows):
    n = product.shape[0]
    diagonal = lax.broadcasted_iota(jnp.int32, (n, n), 0) == lax.broadcasted_iota(jnp.int32, (n, n), 1)
    return product * f32(1 / rows) + jnp.where(diagonal, f32(ridge), f32(0))


def gram_of(blocks):
    product = sum(lax.dot_general(b, b, column_dims, preferred_element_type=f32) for b in blocks)
    return shifted(product, sum(b.shape[0] for b in blocks))


def log_pivots(grams, place=None, cand=None):
    sets, n = len(grams), grams[0].shape[0]
    operands, specs = list(grams), [pl.BlockSpec(memory_space=pltpu.VMEM)] * sets
    if cand is not None:
        operands += [place[None], cand]
        specs += [pl.BlockSpec(memory_space=pltpu.SMEM), pl.BlockSpec(memory_space=pltpu.VMEM)]
    return pl.pallas_call(
        functools.partial(pivots_kernel, sets, cand is not None),
        out_shape=jax.ShapeDtypeStruct((1, n), f32),
        in_specs=specs,
        out_specs=pl.BlockSpec(memory_space=pltpu.VMEM),
        scratch_shapes=[pltpu.VMEM((n, n), f32)] * sets + [pltpu.VMEM((sets, n), f32)],
        compiler_params=pltpu.CompilerParams(vmem_limit_bytes=40 << 20),
    )(*operands)


def half_of(block, upper):
    size = block.shape[-1] // 2
    return lax.dynamic_slice_in_dim(block, upper * size, size, axis=block.ndim - 1)


def sketch_kernel(mode, columns, starts, dots, plain, *refs):
    refs, out_ref = refs[:-1], refs[-1]
    mixes, refs = refs[:dots], refs[dots:]
    views = [ref.at[:, start : start + columns] for ref, start in zip(refs, starts)]
    points, terms, coded = views[:dots], views[dots : dots + plain], views[dots + plain :]
    size = {"code": out_ref.shape[0] - tag_rows, "keep": out_ref.shape[0], "multiply": 2 * out_ref.shape[0]}[mode] // 2
    totals = []
    for i in range(2):
        own, total = pl.ds(i * size, size), 0.0
        for mix_ref, points_ref in zip(mixes, points):
            total += lax.dot_general(mix_ref[i], points_ref[...], column_dims, preferred_element_type=f32)
        for term in terms:
            total += term[own, :]
        for codes in coded:
            total += codes[own, :] * jnp.exp2(codes[2 * size : 2 * size + 1, :] - top)
        totals.append(total)
    if mode == "code":
        largest = jnp.maximum(*[jnp.max(jnp.abs(t), axis=(0, 1), keepdims=True) for t in totals])
        exponent = jnp.ceil(jnp.log2(jnp.maximum(largest, f32(1e-30))))
        totals = [total * jnp.exp2(top - exponent) for total in totals]
        out_ref[2 * size :, :] = jnp.broadcast_to(exponent, (tag_rows, columns))
    if mode == "multiply":
        out_ref[...] = (totals[0] * totals[1]).astype(bf16)
    else:
        for i in range(2):
            out_ref[i * size : (i + 1) * size, :] = totals[i]


def sketch(mode, block, mixes, plain=()):
    columns, points, coded = block
    size = mixes[0].shape[2]
    rows, kind = {"code": (2 * size + tag_rows, f32), "keep": (2 * size, f32), "multiply": (size, bf16)}[mode]
    terms = list(points) + list(plain) + list(coded)
    operands = list(mixes[: len(points)]) + [array for array, _ in terms]
    return pl.pallas_call(
        functools.partial(sketch_kernel, mode, columns, [start for _, start in terms], len(points), len(plain)),
        out_shape=jax.ShapeDtypeStruct((rows, columns), kind),
        in_specs=[pl.BlockSpec(memory_space=pltpu.VMEM)] * len(operands),
        out_specs=pl.BlockSpec(memory_space=pltpu.VMEM),
        compiler_params=pltpu.CompilerParams(vmem_limit_bytes=48 << 20),
    )(*operands)


def halves(block):
    size = block[0] // 2
    return [[size] + [[(a, first + shift) for a, first in terms] for terms in block[1:]] for shift in (0, size)]


def local(orbitals, w_first, w_second, pivots):
    here, place = lax.axis_index("grid"), lax.axis_index("band")
    groups = lax.axis_size("grid")
    grid_bits, band_bits = bits_of(groups), bits_of(lax.axis_size("band"))
    order = pivots[0]
    kept = order.shape[1]
    width = orbitals.shape[1] // groups

    parts = 2 if grid_bits > 1 else 1
    count = groups // 2 // parts
    places = [[reversed_bits(p * count + i, grid_bits - 1) for i in range(count)] for p in range(parts)]

    def blocks_of(p, side):
        return [
            lax.dynamic_slice_in_dim(orbitals, (here ^ 2 * k + side) * width, width, axis=1) for k in places[p]
        ]

    raw = jnp.concatenate(blocks_of(parts - 1, 1), axis=1)
    raw, orders = lax.optimization_barrier((raw, order[:1]))
    raw = exchange(raw, "grid", 1)

    mixing = [jnp.stack([w_first, w_second])]
    for t in reversed(range(1, band_bits)):
        upper = place >> t & 1
        got = [exchange(half_of(m, 1 - upper), "band", 1 << t) for m in mixing]
        mixing = [half_of(m, upper) for m in mixing] + got
    near = mixing[0]

    for t in reversed(range(2, grid_bits)):
        orders = jnp.stack([orders, exchange(orders, "grid", 1 << t)], axis=1).reshape(-1, kept)
    if parts > 1:
        listed = jnp.concatenate([orders[k >> 1] for k in places[0]])
        size, span = near.shape[1:]
        digits = jnp.stack([listed >> 8, listed & 255]).astype(bf16)
        digits = jnp.pad(digits, ((0, 0), (0, -listed.shape[0] % (16 * span)))).reshape(2, -1, span)
        near = exchange(jnp.concatenate([near, digits], axis=1), "grid", 1)
        near, digits = near[:, :size], near[:, size:].reshape(2, -1)[:, : listed.shape[0]].astype(jnp.int32)
        far_lists = (digits[0] * 256 + digits[1]).reshape(-1, kept)
        orders = jnp.stack([orders, exchange(orders, "grid", 2)], axis=1).reshape(-1, kept)
    else:
        near = exchange(near, "grid", 1)
    near = [near] + [exchange(m, "grid", 1) for m in mixing[1:]]

    def over_bands(block):
        blocks = [block]
        for t in reversed(range(1, band_bits)):
            blocks = blocks + [exchange(m, "band", 1 << t) for m in blocks]
        return blocks

    def joined(rows):
        return jnp.concatenate(over_bands(rows), axis=0)

    def over_cores(rows):
        return [rows, exchange(rows, "band", 1)]

    def shares(matrices):
        whole = jnp.concatenate(matrices, axis=1)
        return [half_of(whole, place & 1), exchange(half_of(whole, 1 - (place & 1)), "band", 1)]

    own = pick([block for p in range(parts) for block in blocks_of(p, 0)], [orders[k] for p in places for k in p])
    far = [None] * parts
    far[-1] = pick([raw[:, i * width : (i + 1) * width] for i in range(count)], [orders[k] for k in places[-1]])
    if parts > 1:
        far[0] = exchange(pick(blocks_of(0, 1), far_lists), "grid", 1)
    own = over_cores(joined(own))
    mixes = shares(mixing) + shares(near)

    def block_of(p, rows):
        columns = count * kept
        return [columns, [(array, p * columns) for array in own] + [(array, 0) for array in over_cores(rows)], []]

    go = block_of(parts - 1, joined(far[-1]))

    if parts > 1:
        stay = None
        for t in range(1, grid_bits):
            pieces = halves(go) if t < grid_bits - 1 else [go]
            codes = [sketch("code", piece, mixes).astype(f16) for piece in reversed(pieces)]
            got = exchange(codes[0], "grid", 1 << t)
            if stay is None:
                codes[1:], rows = lax.optimization_barrier((codes[1:], far[0]))
                got, rows = lax.optimization_barrier((got, joined(rows)))
                stay = block_of(0, rows)
            if len(pieces) > 1:
                stay, go = halves(stay)
                go[2].append((got.astype(f32), 0))
                stay[2].append((exchange(codes[1], "grid", 1 << t).astype(f32), 0))
        held = sketch("keep", stay, mixes)
        chosen = sketch("multiply", [kept, [], [(got.astype(f32), 0)]], mixes, [(held, 0)])
    else:
        chosen = sketch("multiply", go, mixes)

    def in_order(block, got, t):
        upper = place >> t & 1 == 1
        count = 1 << (band_bits - 1 - t)
        share = block.reshape((count, -1) + block.shape[1:])
        other = got.reshape(share.shape)
        low, high = jnp.where(upper, other, share), jnp.where(upper, share, other)
        return jnp.concatenate([low, high], axis=1).reshape((-1,) + block.shape[1:])

    def over_higher(block):
        for t in reversed(range(1, band_bits)):
            block = in_order(block, exchange(block, "band", 1 << t), t)
        return block

    rounds = grid_bits + 1
    paired = rounds - 2 + rounds % 2
    index = lax.broadcasted_iota(jnp.int32, (kept, kept), 0)
    even = place & 1 == 0
    shared, grams = [], []
    for section in range(rounds):
        if section:
            got = exchange(chosen, "grid", 1 << section - 1)
            upper = here >> section - 1 & 1
            mine = (index == order[section] - upper * kept).astype(bf16)
            other = (index == order[section] - (1 - upper) * kept).astype(bf16)
            chosen = jnp.dot(chosen, mine, preferred_element_type=f32) + jnp.dot(got, other, preferred_element_type=f32)
            chosen = chosen.astype(bf16)
        if section == rounds - 1:
            final = over_higher(chosen)
        else:
            block = chosen
            if shared:
                block, shared[-1] = lax.optimization_barrier((block, shared[-1]))
            shared.append(over_higher(block))
            if section < paired and section % 2:
                low, high = shared[-2:]
                got = exchange(jnp.where(even, high, low), "band", 1)
                grams.append(gram_of([jnp.where(even, low, high), got]))
    cands = in_order(final, exchange(final, "band", 1), 0)
    if rounds % 2:
        odd = log_pivots([gram_of([cands])])
        quality = jnp.where(even, 0.0, odd) + (log_pivots(grams) if grams else 0.0)
    else:
        last = gram_of([shared[-1], exchange(shared[-1], "band", 1)])
        quality = log_pivots(grams + [last], place, cands)
    return cands, quality + exchange(quality, "band", 1)


def solution(mesh):
    in_specs = (
        P(("band", "grid"), None),
        P(("band", "grid"), None),
        P(("band", "grid"), None),
        P("grid", None, None),
    )
    out_specs = (P(), P("grid", None))
    return jax.shard_map(local, mesh=mesh, in_specs=in_specs, out_specs=out_specs, check_vma=False)
```

```python
import functools

import jax
import jax.numpy as jnp
from jax import lax
from jax.experimental import pallas as pl
from jax.experimental.pallas import tpu as pltpu
from jax.sharding import PartitionSpec as P

ridge = 0.1
f32, bf16, f16 = jnp.float32, jnp.bfloat16, jnp.float16
step, height, lanes = 8, 64, 128
top, tag_rows = 14.0, 16
column_dims = (((0,), (0,)), ((), ()))


def bits_of(count):
    return count.bit_length() - 1


def exchange(block, axis, delta):
    count = lax.axis_size(axis)
    return lax.ppermute(block, axis, [(i, i ^ delta) for i in range(count)])


def reversed_bits(value, bits):
    out = 0
    for t in range(bits):
        out = out | ((value >> t) & 1) << (bits - 1 - t)
    return out


def pick(blocks, lists):
    out = []
    for block, listed in zip(blocks, lists):
        index = lax.broadcasted_iota(jnp.int32, (block.shape[1], listed.shape[0]), 0)
        one_hot = (index == listed).astype(bf16)
        out.append(jnp.dot(block, one_hot, preferred_element_type=f32).astype(bf16))
    return jnp.concatenate(out, axis=1)


def split3(v):
    a = v.astype(bf16)
    rest = v - a.astype(f32)
    b = rest.astype(bf16)
    c = (rest - b.astype(f32)).astype(bf16)
    return a, b, c


def eliminate(block, first):
    width = min(lanes, block.shape[1])
    lane = lax.broadcasted_iota(jnp.int32, (1, width), 1)
    on_diagonal = lax.broadcasted_iota(jnp.int32, (step, width), 1) - lax.broadcasted_iota(
        jnp.int32, (step, width), 0
    )
    done, scaled, diagonal = [], [], 0.0
    for corner in range(0, block.shape[0], step):
        below = lax.broadcasted_iota(jnp.int32, (block.shape[0], 1), 0)
        start = first + corner
        near = block[:, :width]
        columns = [jnp.sum(jnp.where(lane == start + j, near, 0.0), axis=1, keepdims=True) for j in range(step)]
        heads, inverses = [], []
        for j in range(step):
            head = columns[j][j : j + 1, :]
            inverse = 1.0 / head
            factor = jnp.where(below > j, columns[j] * inverse, 0.0)
            block = block - factor * block[j : j + 1, :]
            for c in range(j + 1, step):
                columns[c] = columns[c] - factor * columns[c][j : j + 1, :]
            heads.append(head)
            inverses.append(inverse)
        heads = jnp.concatenate(heads, axis=0)
        diagonal = diagonal + jnp.sum(jnp.where(on_diagonal == start, heads, 0.0), axis=0, keepdims=True)
        done.append(block[:step])
        scaled.append(block[:step] * jnp.concatenate(inverses, axis=0))
        block = block[step:]
    return jnp.concatenate(done, axis=0), jnp.concatenate(scaled, axis=0), diagonal


def outer(scaled, rows):
    u1, u2, u3 = split3(rows)
    v1, v2, v3 = split3(scaled)
    left = jnp.concatenate([v1, v1, v2, v2, v1, v3], axis=0)
    right = jnp.concatenate([u1, u2, u1, u2, u3, u1], axis=0)
    return lax.dot_general(left, right, column_dims, preferred_element_type=f32)


def pivots_kernel(sets, late, *refs):
    grams, refs = refs[:sets], refs[sets:]
    if late:
        place_ref, cand_ref, refs = refs[0], refs[1], refs[2:]
    total_ref, work, diagonals = refs[0], refs[1:-1], refs[-1]
    n = grams[0].shape[0]
    for gram, matrix in zip(grams, work):
        matrix[...] = gram[...]
    if late:
        product = lax.dot_general(cand_ref[...], cand_ref[...], column_dims, preferred_element_type=f32)
        last = work[-1]
        last[...] = jnp.where(place_ref[0] & 1 == 0, last[...], shifted(product, cand_ref.shape[0]))
    diagonals[...] = jnp.zeros_like(diagonals)
    for base in range(0, n, lanes):

        def panel(k, carry, base=base):
            first = pl.multiple_of(k * height, height)
            parts = [eliminate(matrix[pl.ds(base + first, height), base:], first) for matrix in work]
            for q, (done, scaled, diagonal) in enumerate(parts):
                diagonals[q : q + 1, base : base + diagonal.shape[1]] += diagonal
                work[q][base:, base:] -= outer(scaled, done)
            return carry

        lax.fori_loop(0, min(lanes, n - base) // height, panel, 0)
    total_ref[...] = jnp.sum(0.5 * jnp.log(diagonals[...]), axis=0, keepdims=True)


def shifted(product, rows):
    n = product.shape[0]
    diagonal = lax.broadcasted_iota(jnp.int32, (n, n), 0) == lax.broadcasted_iota(jnp.int32, (n, n), 1)
    return product * f32(1 / rows) + jnp.where(diagonal, f32(ridge), f32(0))


def gram_of(blocks):
    product = sum(lax.dot_general(b, b, column_dims, preferred_element_type=f32) for b in blocks)
    return shifted(product, sum(b.shape[0] for b in blocks))


def log_pivots(grams, place=None, cand=None):
    sets, n = len(grams), grams[0].shape[0]
    operands, specs = list(grams), [pl.BlockSpec(memory_space=pltpu.VMEM)] * sets
    if cand is not None:
        operands += [place[None], cand]
        specs += [pl.BlockSpec(memory_space=pltpu.SMEM), pl.BlockSpec(memory_space=pltpu.VMEM)]
    return pl.pallas_call(
        functools.partial(pivots_kernel, sets, cand is not None),
        out_shape=jax.ShapeDtypeStruct((1, n), f32),
        in_specs=specs,
        out_specs=pl.BlockSpec(memory_space=pltpu.VMEM),
        scratch_shapes=[pltpu.VMEM((n, n), f32)] * sets + [pltpu.VMEM((sets, n), f32)],
        compiler_params=pltpu.CompilerParams(vmem_limit_bytes=40 << 20),
    )(*operands)


def half_of(block, upper):
    size = block.shape[-1] // 2
    return lax.dynamic_slice_in_dim(block, upper * size, size, axis=block.ndim - 1)


def sketch_kernel(mode, columns, starts, dots, plain, *refs):
    refs, out_ref = refs[:-1], refs[-1]
    mixes, refs = refs[:dots], refs[dots:]
    views = [ref.at[:, start : start + columns] for ref, start in zip(refs, starts)]
    points, terms, coded = views[:dots], views[dots : dots + plain], views[dots + plain :]
    size = {"code": out_ref.shape[0] - tag_rows, "keep": out_ref.shape[0], "multiply": 2 * out_ref.shape[0]}[mode] // 2
    totals = []
    for i in range(2):
        own, total = pl.ds(i * size, size), 0.0
        for mix_ref, points_ref in zip(mixes, points):
            total += lax.dot_general(mix_ref[i], points_ref[...], column_dims, preferred_element_type=f32)
        for term in terms:
            total += term[own, :]
        for codes in coded:
            total += codes[own, :] * jnp.exp2(codes[2 * size : 2 * size + 1, :] - top)
        totals.append(total)
    if mode == "code":
        largest = jnp.maximum(*[jnp.max(jnp.abs(t), axis=(0, 1), keepdims=True) for t in totals])
        exponent = jnp.ceil(jnp.log2(jnp.maximum(largest, f32(1e-30))))
        totals = [total * jnp.exp2(top - exponent) for total in totals]
        out_ref[2 * size :, :] = jnp.broadcast_to(exponent, (tag_rows, columns))
    if mode == "multiply":
        out_ref[...] = (totals[0] * totals[1]).astype(bf16)
    else:
        for i in range(2):
            out_ref[i * size : (i + 1) * size, :] = totals[i]


def sketch(mode, block, mixes, plain=()):
    columns, points, coded = block
    size = mixes[0].shape[2]
    rows, kind = {"code": (2 * size + tag_rows, f32), "keep": (2 * size, f32), "multiply": (size, bf16)}[mode]
    terms = list(points) + list(plain) + list(coded)
    operands = list(mixes[: len(points)]) + [array for array, _ in terms]
    return pl.pallas_call(
        functools.partial(sketch_kernel, mode, columns, [start for _, start in terms], len(points), len(plain)),
        out_shape=jax.ShapeDtypeStruct((rows, columns), kind),
        in_specs=[pl.BlockSpec(memory_space=pltpu.VMEM)] * len(operands),
        out_specs=pl.BlockSpec(memory_space=pltpu.VMEM),
        compiler_params=pltpu.CompilerParams(vmem_limit_bytes=48 << 20),
    )(*operands)


def halves(block):
    size = block[0] // 2
    return [[size] + [[(a, first + shift) for a, first in terms] for terms in block[1:]] for shift in (0, size)]


def local(orbitals, w_first, w_second, pivots):
    here, place = lax.axis_index("grid"), lax.axis_index("band")
    groups = lax.axis_size("grid")
    grid_bits, band_bits = bits_of(groups), bits_of(lax.axis_size("band"))
    order = pivots[0]
    kept = order.shape[1]
    width = orbitals.shape[1] // groups

    parts = 2 if grid_bits > 1 else 1
    count = groups // 2 // parts
    places = [[reversed_bits(p * count + i, grid_bits - 1) for i in range(count)] for p in range(parts)]

    def blocks_of(p, side):
        return [
            lax.dynamic_slice_in_dim(orbitals, (here ^ 2 * k + side) * width, width, axis=1) for k in places[p]
        ]

    raw = jnp.concatenate(blocks_of(parts - 1, 1), axis=1)
    raw, orders = lax.optimization_barrier((raw, order[:1]))
    raw = exchange(raw, "grid", 1)

    mixing = [jnp.stack([w_first, w_second])]
    for t in reversed(range(1, band_bits)):
        upper = place >> t & 1
        got = [exchange(half_of(m, 1 - upper), "band", 1 << t) for m in mixing]
        mixing = [half_of(m, upper) for m in mixing] + got
    near = mixing[0]

    for t in reversed(range(2, grid_bits)):
        orders = jnp.stack([orders, exchange(orders, "grid", 1 << t)], axis=1).reshape(-1, kept)
    if parts > 1:
        listed = jnp.concatenate([orders[k >> 1] for k in places[0]])
        size, span = near.shape[1:]
        digits = jnp.stack([listed >> 8, listed & 255]).astype(bf16)
        digits = jnp.pad(digits, ((0, 0), (0, -listed.shape[0] % (16 * span)))).reshape(2, -1, span)
        near = exchange(jnp.concatenate([near, digits], axis=1), "grid", 1)
        near, digits = near[:, :size], near[:, size:].reshape(2, -1)[:, : listed.shape[0]].astype(jnp.int32)
        far_lists = (digits[0] * 256 + digits[1]).reshape(-1, kept)
        orders = jnp.stack([orders, exchange(orders, "grid", 2)], axis=1).reshape(-1, kept)
    else:
        near = exchange(near, "grid", 1)
    near = [near] + [exchange(m, "grid", 1) for m in mixing[1:]]

    def over_bands(block):
        blocks = [block]
        for t in reversed(range(1, band_bits)):
            blocks = blocks + [exchange(m, "band", 1 << t) for m in blocks]
        return blocks

    def joined(rows):
        return jnp.concatenate(over_bands(rows), axis=0)

    def over_cores(rows):
        return [rows, exchange(rows, "band", 1)]

    def shares(matrices):
        whole = jnp.concatenate(matrices, axis=1)
        return [half_of(whole, place & 1), exchange(half_of(whole, 1 - (place & 1)), "band", 1)]

    own = pick([block for p in range(parts) for block in blocks_of(p, 0)], [orders[k] for p in places for k in p])
    far = [None] * parts
    far[-1] = pick([raw[:, i * width : (i + 1) * width] for i in range(count)], [orders[k] for k in places[-1]])
    if parts > 1:
        far[0] = pick(blocks_of(0, 1), far_lists)
        far[0], near = lax.optimization_barrier((far[0], near))
        far[0] = exchange(far[0], "grid", 1)
    own = over_cores(joined(own))
    mixes = shares(mixing) + shares(near)

    def block_of(p, rows):
        columns = count * kept
        return [columns, [(array, p * columns) for array in own] + [(array, 0) for array in over_cores(rows)], []]

    go = block_of(parts - 1, joined(far[-1]))

    if parts > 1:
        stay = None
        for t in range(1, grid_bits):
            pieces = halves(go) if t < grid_bits - 1 else [go]
            codes = [sketch("code", piece, mixes).astype(f16) for piece in reversed(pieces)]
            got = exchange(codes[0], "grid", 1 << t)
            if stay is None:
                codes[1:], rows = lax.optimization_barrier((codes[1:], far[0]))
                got, rows = lax.optimization_barrier((got, joined(rows)))
                stay = block_of(0, rows)
            if len(pieces) > 1:
                stay, go = halves(stay)
                go[2].append((got.astype(f32), 0))
                stay[2].append((exchange(codes[1], "grid", 1 << t).astype(f32), 0))
        held = sketch("keep", stay, mixes)
        chosen = sketch("multiply", [kept, [], [(got.astype(f32), 0)]], mixes, [(held, 0)])
    else:
        chosen = sketch("multiply", go, mixes)

    def in_order(block, got, t):
        upper = place >> t & 1 == 1
        count = 1 << (band_bits - 1 - t)
        share = block.reshape((count, -1) + block.shape[1:])
        other = got.reshape(share.shape)
        low, high = jnp.where(upper, other, share), jnp.where(upper, share, other)
        return jnp.concatenate([low, high], axis=1).reshape((-1,) + block.shape[1:])

    def over_higher(block):
        for t in reversed(range(1, band_bits)):
            block = in_order(block, exchange(block, "band", 1 << t), t)
        return block

    rounds = grid_bits + 1
    paired = rounds - 2 + rounds % 2
    index = lax.broadcasted_iota(jnp.int32, (kept, kept), 0)
    even = place & 1 == 0
    shared, grams = [], []
    for section in range(rounds):
        if section:
            got = exchange(chosen, "grid", 1 << section - 1)
            upper = here >> section - 1 & 1
            mine = (index == order[section] - upper * kept).astype(bf16)
            other = (index == order[section] - (1 - upper) * kept).astype(bf16)
            chosen = jnp.dot(chosen, mine, preferred_element_type=f32) + jnp.dot(got, other, preferred_element_type=f32)
            chosen = chosen.astype(bf16)
        if section == rounds - 1:
            final = over_higher(chosen)
        else:
            block = chosen
            if shared:
                block, shared[-1] = lax.optimization_barrier((block, shared[-1]))
            shared.append(over_higher(block))
            if section < paired and section % 2:
                low, high = shared[-2:]
                got = exchange(jnp.where(even, high, low), "band", 1)
                grams.append(gram_of([jnp.where(even, low, high), got]))
    cands = in_order(final, exchange(final, "band", 1), 0)
    if rounds % 2:
        odd = log_pivots([gram_of([cands])])
        quality = jnp.where(even, 0.0, odd) + (log_pivots(grams) if grams else 0.0)
    else:
        last = gram_of([shared[-1], exchange(shared[-1], "band", 1)])
        quality = log_pivots(grams + [last], place, cands)
    return cands, quality + exchange(quality, "band", 1)


def solution(mesh):
    in_specs = (
        P(("band", "grid"), None),
        P(("band", "grid"), None),
        P(("band", "grid"), None),
        P("grid", None, None),
    )
    out_specs = (P(), P("grid", None))
    return jax.shard_map(local, mesh=mesh, in_specs=in_specs, out_specs=out_specs, check_vma=False)
```

```python
import functools

import jax
import jax.numpy as jnp
from jax import lax
from jax.experimental import pallas as pl
from jax.experimental.pallas import tpu as pltpu
from jax.sharding import PartitionSpec as P

ridge = 0.1
f32, bf16, f16 = jnp.float32, jnp.bfloat16, jnp.float16
step, height, lanes = 8, 64, 128
top, tag_rows = 14.0, 16
column_dims = (((0,), (0,)), ((), ()))


def bits_of(count):
    return count.bit_length() - 1


def exchange(block, axis, delta):
    count = lax.axis_size(axis)
    return lax.ppermute(block, axis, [(i, i ^ delta) for i in range(count)])


def reversed_bits(value, bits):
    out = 0
    for t in range(bits):
        out = out | ((value >> t) & 1) << (bits - 1 - t)
    return out


def pick(blocks, lists):
    out = []
    for block, listed in zip(blocks, lists):
        index = lax.broadcasted_iota(jnp.int32, (block.shape[1], listed.shape[0]), 0)
        one_hot = (index == listed).astype(bf16)
        out.append(jnp.dot(block, one_hot, preferred_element_type=f32).astype(bf16))
    return jnp.concatenate(out, axis=1)


def split3(v):
    a = v.astype(bf16)
    rest = v - a.astype(f32)
    b = rest.astype(bf16)
    c = (rest - b.astype(f32)).astype(bf16)
    return a, b, c


def eliminate(block, first):
    width = min(lanes, block.shape[1])
    lane = lax.broadcasted_iota(jnp.int32, (1, width), 1)
    on_diagonal = lax.broadcasted_iota(jnp.int32, (step, width), 1) - lax.broadcasted_iota(
        jnp.int32, (step, width), 0
    )
    done, scaled, diagonal = [], [], 0.0
    for corner in range(0, block.shape[0], step):
        below = lax.broadcasted_iota(jnp.int32, (block.shape[0], 1), 0)
        start = first + corner
        near = block[:, :width]
        columns = [jnp.sum(jnp.where(lane == start + j, near, 0.0), axis=1, keepdims=True) for j in range(step)]
        heads, inverses = [], []
        for j in range(step):
            head = columns[j][j : j + 1, :]
            inverse = 1.0 / head
            factor = jnp.where(below > j, columns[j] * inverse, 0.0)
            block = block - factor * block[j : j + 1, :]
            for c in range(j + 1, step):
                columns[c] = columns[c] - factor * columns[c][j : j + 1, :]
            heads.append(head)
            inverses.append(inverse)
        heads = jnp.concatenate(heads, axis=0)
        diagonal = diagonal + jnp.sum(jnp.where(on_diagonal == start, heads, 0.0), axis=0, keepdims=True)
        done.append(block[:step])
        scaled.append(block[:step] * jnp.concatenate(inverses, axis=0))
        block = block[step:]
    return jnp.concatenate(done, axis=0), jnp.concatenate(scaled, axis=0), diagonal


def outer(scaled, rows):
    u1, u2, u3 = split3(rows)
    v1, v2, v3 = split3(scaled)
    left = jnp.concatenate([v1, v1, v2, v2, v1, v3], axis=0)
    right = jnp.concatenate([u1, u2, u1, u2, u3, u1], axis=0)
    return lax.dot_general(left, right, column_dims, preferred_element_type=f32)


def pivots_kernel(sets, late, *refs):
    grams, refs = refs[:sets], refs[sets:]
    if late:
        place_ref, part_ref, cand_ref, refs = refs[0], refs[1], refs[2], refs[3:]
    total_ref, work, diagonals = refs[0], refs[1:-1], refs[-1]
    n = grams[0].shape[0]
    for gram, matrix in zip(grams, work):
        matrix[...] = gram[...]
    if late:
        product = 0.0
        for half in (part_ref, cand_ref):
            product += lax.dot_general(half[...], half[...], column_dims, preferred_element_type=f32)
        last = work[-1]
        product = shifted(product, 2 * cand_ref.shape[0])
        last[...] = jnp.where(place_ref[0] & 1 == 0, last[...], product)
    diagonals[...] = jnp.zeros_like(diagonals)
    for base in range(0, n, lanes):

        def panel(k, carry, base=base):
            first = pl.multiple_of(k * height, height)
            parts = [eliminate(matrix[pl.ds(base + first, height), base:], first) for matrix in work]
            for q, (done, scaled, diagonal) in enumerate(parts):
                diagonals[q : q + 1, base : base + diagonal.shape[1]] += diagonal
                work[q][base:, base:] -= outer(scaled, done)
            return carry

        lax.fori_loop(0, min(lanes, n - base) // height, panel, 0)
    total_ref[...] = jnp.sum(0.5 * jnp.log(diagonals[...]), axis=0, keepdims=True)


def shifted(product, rows):
    n = product.shape[0]
    diagonal = lax.broadcasted_iota(jnp.int32, (n, n), 0) == lax.broadcasted_iota(jnp.int32, (n, n), 1)
    return product * f32(1 / rows) + jnp.where(diagonal, f32(ridge), f32(0))


def gram_of(blocks):
    product = sum(lax.dot_general(b, b, column_dims, preferred_element_type=f32) for b in blocks)
    return shifted(product, sum(b.shape[0] for b in blocks))


def log_pivots(grams, place=None, part=None, cand=None):
    sets, n = len(grams), grams[0].shape[0]
    operands, specs = list(grams), [pl.BlockSpec(memory_space=pltpu.VMEM)] * sets
    if cand is not None:
        operands += [place[None], part, cand]
        specs += [pl.BlockSpec(memory_space=pltpu.SMEM)] + [pl.BlockSpec(memory_space=pltpu.VMEM)] * 2
    return pl.pallas_call(
        functools.partial(pivots_kernel, sets, cand is not None),
        out_shape=jax.ShapeDtypeStruct((1, n), f32),
        in_specs=specs,
        out_specs=pl.BlockSpec(memory_space=pltpu.VMEM),
        scratch_shapes=[pltpu.VMEM((n, n), f32)] * sets + [pltpu.VMEM((sets, n), f32)],
        compiler_params=pltpu.CompilerParams(vmem_limit_bytes=40 << 20),
    )(*operands)


def half_of(block, upper):
    size = block.shape[-1] // 2
    return lax.dynamic_slice_in_dim(block, upper * size, size, axis=block.ndim - 1)


def sketch_kernel(mode, columns, starts, dots, plain, *refs):
    refs, out_ref = refs[:-1], refs[-1]
    mixes, refs = refs[:dots], refs[dots:]
    views = [ref.at[:, start : start + columns] for ref, start in zip(refs, starts)]
    points, terms, coded = views[:dots], views[dots : dots + plain], views[dots + plain :]
    size = {"code": out_ref.shape[0] - tag_rows, "keep": out_ref.shape[0], "multiply": 2 * out_ref.shape[0]}[mode] // 2
    totals = []
    for i in range(2):
        own, total = pl.ds(i * size, size), 0.0
        for mix_ref, points_ref in zip(mixes, points):
            total += lax.dot_general(mix_ref[i], points_ref[...], column_dims, preferred_element_type=f32)
        for term in terms:
            total += term[own, :]
        for codes in coded:
            total += codes[own, :] * jnp.exp2(codes[2 * size : 2 * size + 1, :] - top)
        totals.append(total)
    if mode == "code":
        largest = jnp.maximum(*[jnp.max(jnp.abs(t), axis=(0, 1), keepdims=True) for t in totals])
        exponent = jnp.ceil(jnp.log2(jnp.maximum(largest, f32(1e-30))))
        totals = [total * jnp.exp2(top - exponent) for total in totals]
        out_ref[2 * size :, :] = jnp.broadcast_to(exponent, (tag_rows, columns))
    if mode == "multiply":
        out_ref[...] = (totals[0] * totals[1]).astype(bf16)
    else:
        for i in range(2):
            out_ref[i * size : (i + 1) * size, :] = totals[i]


def sketch(mode, block, mixes, plain=()):
    columns, points, coded = block
    size = mixes[0].shape[2]
    rows, kind = {"code": (2 * size + tag_rows, f32), "keep": (2 * size, f32), "multiply": (size, bf16)}[mode]
    terms = list(points) + list(plain) + list(coded)
    operands = list(mixes[: len(points)]) + [array for array, _ in terms]
    return pl.pallas_call(
        functools.partial(sketch_kernel, mode, columns, [start for _, start in terms], len(points), len(plain)),
        out_shape=jax.ShapeDtypeStruct((rows, columns), kind),
        in_specs=[pl.BlockSpec(memory_space=pltpu.VMEM)] * len(operands),
        out_specs=pl.BlockSpec(memory_space=pltpu.VMEM),
        compiler_params=pltpu.CompilerParams(vmem_limit_bytes=48 << 20),
    )(*operands)


def halves(block):
    size = block[0] // 2
    return [[size] + [[(a, first + shift) for a, first in terms] for terms in block[1:]] for shift in (0, size)]


def local(orbitals, w_first, w_second, pivots):
    here, place = lax.axis_index("grid"), lax.axis_index("band")
    groups = lax.axis_size("grid")
    grid_bits, band_bits = bits_of(groups), bits_of(lax.axis_size("band"))
    order = pivots[0]
    kept = order.shape[1]
    width = orbitals.shape[1] // groups

    parts = 2 if grid_bits > 1 else 1
    count = groups // 2 // parts
    places = [[reversed_bits(p * count + i, grid_bits - 1) for i in range(count)] for p in range(parts)]

    def blocks_of(p, side):
        return [
            lax.dynamic_slice_in_dim(orbitals, (here ^ 2 * k + side) * width, width, axis=1) for k in places[p]
        ]

    raw = jnp.concatenate(blocks_of(parts - 1, 1), axis=1)
    raw, orders = lax.optimization_barrier((raw, order[:1]))
    raw = exchange(raw, "grid", 1)

    mixing = [jnp.stack([w_first, w_second])]
    for t in reversed(range(1, band_bits)):
        upper = place >> t & 1
        got = [exchange(half_of(m, 1 - upper), "band", 1 << t) for m in mixing]
        mixing = [half_of(m, upper) for m in mixing] + got
    near = mixing[0]

    for t in reversed(range(2, grid_bits)):
        orders = jnp.stack([orders, exchange(orders, "grid", 1 << t)], axis=1).reshape(-1, kept)
    if parts > 1:
        listed = jnp.concatenate([orders[k >> 1] for k in places[0]])
        size, span = near.shape[1:]
        digits = jnp.stack([listed >> 8, listed & 255]).astype(bf16)
        digits = jnp.pad(digits, ((0, 0), (0, -listed.shape[0] % (16 * span)))).reshape(2, -1, span)
        near = exchange(jnp.concatenate([near, digits], axis=1), "grid", 1)
        near, digits = near[:, :size], near[:, size:].reshape(2, -1)[:, : listed.shape[0]].astype(jnp.int32)
        far_lists = (digits[0] * 256 + digits[1]).reshape(-1, kept)
        orders = jnp.stack([orders, exchange(orders, "grid", 2)], axis=1).reshape(-1, kept)
    else:
        near = exchange(near, "grid", 1)
    near = [near] + [exchange(m, "grid", 1) for m in mixing[1:]]

    def over_bands(block):
        blocks = [block]
        for t in reversed(range(1, band_bits)):
            blocks = blocks + [exchange(m, "band", 1 << t) for m in blocks]
        return blocks

    def joined(rows):
        return jnp.concatenate(over_bands(rows), axis=0)

    def over_cores(rows):
        return [rows, exchange(rows, "band", 1)]

    def shares(matrices):
        whole = jnp.concatenate(matrices, axis=1)
        return [half_of(whole, place & 1), exchange(half_of(whole, 1 - (place & 1)), "band", 1)]

    own = pick([block for p in range(parts) for block in blocks_of(p, 0)], [orders[k] for p in places for k in p])
    far = [None] * parts
    far[-1] = pick([raw[:, i * width : (i + 1) * width] for i in range(count)], [orders[k] for k in places[-1]])
    if parts > 1:
        far[0] = pick(blocks_of(0, 1), far_lists)
        far[0], near = lax.optimization_barrier((far[0], near))
        far[0] = exchange(far[0], "grid", 1)
    own = over_cores(joined(own))
    mixes = shares(mixing) + shares(near)

    def block_of(p, rows):
        columns = count * kept
        return [columns, [(array, p * columns) for array in own] + [(array, 0) for array in over_cores(rows)], []]

    go = block_of(parts - 1, joined(far[-1]))

    if parts > 1:
        stay = None
        for t in range(1, grid_bits):
            pieces = halves(go) if t < grid_bits - 1 else [go]
            codes = [sketch("code", piece, mixes).astype(f16) for piece in reversed(pieces)]
            got = exchange(codes[0], "grid", 1 << t)
            if stay is None:
                codes[1:], rows = lax.optimization_barrier((codes[1:], far[0]))
                got, rows = lax.optimization_barrier((got, joined(rows)))
                stay = block_of(0, rows)
            if len(pieces) > 1:
                stay, go = halves(stay)
                go[2].append((got.astype(f32), 0))
                stay[2].append((exchange(codes[1], "grid", 1 << t).astype(f32), 0))
        held = sketch("keep", stay, mixes)
        chosen = sketch("multiply", [kept, [], [(got.astype(f32), 0)]], mixes, [(held, 0)])
    else:
        chosen = sketch("multiply", go, mixes)

    def in_order(block, got, t):
        upper = place >> t & 1 == 1
        count = 1 << (band_bits - 1 - t)
        share = block.reshape((count, -1) + block.shape[1:])
        other = got.reshape(share.shape)
        low, high = jnp.where(upper, other, share), jnp.where(upper, share, other)
        return jnp.concatenate([low, high], axis=1).reshape((-1,) + block.shape[1:])

    def over_higher(block):
        for t in reversed(range(1, band_bits)):
            block = in_order(block, exchange(block, "band", 1 << t), t)
        return block

    rounds = grid_bits + 1
    paired = rounds - 2 + rounds % 2
    index = lax.broadcasted_iota(jnp.int32, (kept, kept), 0)
    even = place & 1 == 0
    shared, grams = [], []
    for section in range(rounds):
        if section:
            got = exchange(chosen, "grid", 1 << section - 1)
            upper = here >> section - 1 & 1
            mine = (index == order[section] - upper * kept).astype(bf16)
            other = (index == order[section] - (1 - upper) * kept).astype(bf16)
            chosen = jnp.dot(chosen, mine, preferred_element_type=f32) + jnp.dot(got, other, preferred_element_type=f32)
            chosen = chosen.astype(bf16)
        if section == rounds - 1:
            final = over_higher(chosen)
        else:
            block = chosen
            if shared:
                block, shared[-1] = lax.optimization_barrier((block, shared[-1]))
            shared.append(over_higher(block))
            if section < paired and section % 2:
                low, high = shared[-2:]
                got = exchange(jnp.where(even, high, low), "band", 1)
                grams.append(gram_of([jnp.where(even, low, high), got]))
    got = exchange(final, "band", 1)
    cands = in_order(final, got, 0)
    if rounds % 2:
        odd = log_pivots([gram_of([cands])])
        quality = jnp.where(even, 0.0, odd) + (log_pivots(grams) if grams else 0.0)
    else:
        last = gram_of([shared[-1], exchange(shared[-1], "band", 1)])
        quality = log_pivots(grams + [last], place, final, got)
    return cands, quality + exchange(quality, "band", 1)


def solution(mesh):
    in_specs = (
        P(("band", "grid"), None),
        P(("band", "grid"), None),
        P(("band", "grid"), None),
        P("grid", None, None),
    )
    out_specs = (P(), P("grid", None))
    return jax.shard_map(local, mesh=mesh, in_specs=in_specs, out_specs=out_specs, check_vma=False)
```

```python
import functools

import jax
import jax.numpy as jnp
from jax import lax
from jax.experimental import pallas as pl
from jax.experimental.pallas import tpu as pltpu
from jax.sharding import PartitionSpec as P

ridge = 0.1
f32, bf16, f16 = jnp.float32, jnp.bfloat16, jnp.float16
step, height, lanes = 8, 64, 128
top, tag_rows = 14.0, 16
column_dims = (((0,), (0,)), ((), ()))


def bits_of(count):
    return count.bit_length() - 1


def exchange(block, axis, delta):
    count = lax.axis_size(axis)
    return lax.ppermute(block, axis, [(i, i ^ delta) for i in range(count)])


def reversed_bits(value, bits):
    out = 0
    for t in range(bits):
        out = out | ((value >> t) & 1) << (bits - 1 - t)
    return out


def pick(blocks, lists):
    out = []
    for block, listed in zip(blocks, lists):
        index = lax.broadcasted_iota(jnp.int32, (block.shape[1], listed.shape[0]), 0)
        one_hot = (index == listed).astype(bf16)
        out.append(jnp.dot(block, one_hot, preferred_element_type=f32).astype(bf16))
    return jnp.concatenate(out, axis=1)


def split3(v):
    a = v.astype(bf16)
    rest = v - a.astype(f32)
    b = rest.astype(bf16)
    c = (rest - b.astype(f32)).astype(bf16)
    return a, b, c


def eliminate(block, first):
    width = min(lanes, block.shape[1])
    lane = lax.broadcasted_iota(jnp.int32, (1, width), 1)
    on_diagonal = lax.broadcasted_iota(jnp.int32, (step, width), 1) - lax.broadcasted_iota(
        jnp.int32, (step, width), 0
    )
    done, scaled, diagonal = [], [], 0.0
    for corner in range(0, block.shape[0], step):
        below = lax.broadcasted_iota(jnp.int32, (block.shape[0], 1), 0)
        start = first + corner
        near = block[:, :width]
        columns = [jnp.sum(jnp.where(lane == start + j, near, 0.0), axis=1, keepdims=True) for j in range(step)]
        heads, inverses = [], []
        for j in range(step):
            head = columns[j][j : j + 1, :]
            inverse = 1.0 / head
            factor = jnp.where(below > j, columns[j] * inverse, 0.0)
            block = block - factor * block[j : j + 1, :]
            for c in range(j + 1, step):
                columns[c] = columns[c] - factor * columns[c][j : j + 1, :]
            heads.append(head)
            inverses.append(inverse)
        heads = jnp.concatenate(heads, axis=0)
        diagonal = diagonal + jnp.sum(jnp.where(on_diagonal == start, heads, 0.0), axis=0, keepdims=True)
        done.append(block[:step])
        scaled.append(block[:step] * jnp.concatenate(inverses, axis=0))
        block = block[step:]
    return jnp.concatenate(done, axis=0), jnp.concatenate(scaled, axis=0), diagonal


def outer(scaled, rows):
    u1, u2, u3 = split3(rows)
    v1, v2, v3 = split3(scaled)
    left = jnp.concatenate([v1, v1, v2, v2, v1, v3], axis=0)
    right = jnp.concatenate([u1, u2, u1, u2, u3, u1], axis=0)
    return lax.dot_general(left, right, column_dims, preferred_element_type=f32)


def pivots_kernel(sets, late, *refs):
    grams, refs = refs[:sets], refs[sets:]
    if late:
        place_ref, part_ref, cand_ref, refs = refs[0], refs[1], refs[2], refs[3:]
    total_ref, work, diagonals = refs[0], refs[1:-1], refs[-1]
    n = grams[0].shape[0]
    for gram, matrix in zip(grams, work):
        matrix[...] = gram[...]
    if late:
        product = 0.0
        for half in (part_ref, cand_ref):
            product += lax.dot_general(half[...], half[...], column_dims, preferred_element_type=f32)
        last = work[-1]
        product = shifted(product, 2 * cand_ref.shape[0])
        last[...] = jnp.where(place_ref[0] & 1 == 0, last[...], product)
    diagonals[...] = jnp.zeros_like(diagonals)
    for base in range(0, n, lanes):

        def panel(k, carry, base=base):
            first = pl.multiple_of(k * height, height)
            parts = [eliminate(matrix[pl.ds(base + first, height), base:], first) for matrix in work]
            for q, (done, scaled, diagonal) in enumerate(parts):
                diagonals[q : q + 1, base : base + diagonal.shape[1]] += diagonal
                work[q][base:, base:] -= outer(scaled, done)
            return carry

        lax.fori_loop(0, min(lanes, n - base) // height, panel, 0)
    total_ref[...] = jnp.sum(0.5 * jnp.log(diagonals[...]), axis=0, keepdims=True)


def shifted(product, rows):
    n = product.shape[0]
    diagonal = lax.broadcasted_iota(jnp.int32, (n, n), 0) == lax.broadcasted_iota(jnp.int32, (n, n), 1)
    return product * f32(1 / rows) + jnp.where(diagonal, f32(ridge), f32(0))


def gram_of(blocks):
    product = sum(lax.dot_general(b, b, column_dims, preferred_element_type=f32) for b in blocks)
    return shifted(product, sum(b.shape[0] for b in blocks))


def log_pivots(grams, place=None, part=None, cand=None):
    sets, n = len(grams), grams[0].shape[0]
    operands, specs = list(grams), [pl.BlockSpec(memory_space=pltpu.VMEM)] * sets
    if cand is not None:
        operands += [place[None], part, cand]
        specs += [pl.BlockSpec(memory_space=pltpu.SMEM)] + [pl.BlockSpec(memory_space=pltpu.VMEM)] * 2
    return pl.pallas_call(
        functools.partial(pivots_kernel, sets, cand is not None),
        out_shape=jax.ShapeDtypeStruct((1, n), f32),
        in_specs=specs,
        out_specs=pl.BlockSpec(memory_space=pltpu.VMEM),
        scratch_shapes=[pltpu.VMEM((n, n), f32)] * sets + [pltpu.VMEM((sets, n), f32)],
        compiler_params=pltpu.CompilerParams(vmem_limit_bytes=40 << 20),
    )(*operands)


def half_of(block, upper):
    size = block.shape[-1] // 2
    return lax.dynamic_slice_in_dim(block, upper * size, size, axis=block.ndim - 1)


def sketch_kernel(mode, columns, starts, dots, plain, *refs):
    refs, out_ref = refs[:-1], refs[-1]
    mixes, refs = refs[:dots], refs[dots:]
    views = [ref.at[:, start : start + columns] for ref, start in zip(refs, starts)]
    points, terms, coded = views[:dots], views[dots : dots + plain], views[dots + plain :]
    size = {"code": out_ref.shape[0] - tag_rows, "keep": out_ref.shape[0], "multiply": 2 * out_ref.shape[0]}[mode] // 2
    totals = []
    for i in range(2):
        own, total = pl.ds(i * size, size), 0.0
        for mix_ref, points_ref in zip(mixes, points):
            total += lax.dot_general(mix_ref[i], points_ref[...], column_dims, preferred_element_type=f32)
        for term in terms:
            total += term[own, :]
        for codes in coded:
            total += codes[own, :] * jnp.exp2(codes[2 * size : 2 * size + 1, :] - top)
        totals.append(total)
    if mode == "code":
        largest = jnp.maximum(*[jnp.max(jnp.abs(t), axis=(0, 1), keepdims=True) for t in totals])
        exponent = jnp.ceil(jnp.log2(jnp.maximum(largest, f32(1e-30))))
        totals = [total * jnp.exp2(top - exponent) for total in totals]
        out_ref[2 * size :, :] = jnp.broadcast_to(exponent, (tag_rows, columns))
    if mode == "multiply":
        out_ref[...] = (totals[0] * totals[1]).astype(bf16)
    else:
        for i in range(2):
            out_ref[i * size : (i + 1) * size, :] = totals[i]


def sketch(mode, block, mixes, plain=()):
    columns, points, coded = block
    size = mixes[0].shape[2]
    rows, kind = {"code": (2 * size + tag_rows, f32), "keep": (2 * size, f32), "multiply": (size, bf16)}[mode]
    terms = list(points) + list(plain) + list(coded)
    operands = list(mixes[: len(points)]) + [array for array, _ in terms]
    return pl.pallas_call(
        functools.partial(sketch_kernel, mode, columns, [start for _, start in terms], len(points), len(plain)),
        out_shape=jax.ShapeDtypeStruct((rows, columns), kind),
        in_specs=[pl.BlockSpec(memory_space=pltpu.VMEM)] * len(operands),
        out_specs=pl.BlockSpec(memory_space=pltpu.VMEM),
        compiler_params=pltpu.CompilerParams(vmem_limit_bytes=48 << 20),
    )(*operands)


def halves(block):
    size = block[0] // 2
    return [[size] + [[(a, first + shift) for a, first in terms] for terms in block[1:]] for shift in (0, size)]


def local(orbitals, w_first, w_second, pivots):
    here, place = lax.axis_index("grid"), lax.axis_index("band")
    groups = lax.axis_size("grid")
    grid_bits, band_bits = bits_of(groups), bits_of(lax.axis_size("band"))
    order = pivots[0]
    kept = order.shape[1]
    width = orbitals.shape[1] // groups

    parts = 2 if grid_bits > 1 else 1
    count = groups // 2 // parts
    places = [[reversed_bits(p * count + i, grid_bits - 1) for i in range(count)] for p in range(parts)]

    def blocks_of(p, side):
        return [
            lax.dynamic_slice_in_dim(orbitals, (here ^ 2 * k + side) * width, width, axis=1) for k in places[p]
        ]

    raw = jnp.concatenate(blocks_of(parts - 1, 1), axis=1)
    raw, orders = lax.optimization_barrier((raw, order[:1]))
    raw = exchange(raw, "grid", 1)

    mixing = [jnp.stack([w_first, w_second])]
    for t in reversed(range(1, band_bits)):
        upper = place >> t & 1
        got = [exchange(half_of(m, 1 - upper), "band", 1 << t) for m in mixing]
        mixing = [half_of(m, upper) for m in mixing] + got
    near = mixing[0]

    for t in reversed(range(2, grid_bits)):
        orders = jnp.stack([orders, exchange(orders, "grid", 1 << t)], axis=1).reshape(-1, kept)
    if parts > 1:
        listed = jnp.concatenate([orders[k >> 1] for k in places[0]])
        size, span = near.shape[1:]
        digits = jnp.stack([listed >> 8, listed & 255]).astype(bf16)
        digits = jnp.pad(digits, ((0, 0), (0, -listed.shape[0] % (16 * span)))).reshape(2, -1, span)
        near = exchange(jnp.concatenate([near, digits], axis=1), "grid", 1)
        near, digits = near[:, :size], near[:, size:].reshape(2, -1)[:, : listed.shape[0]].astype(jnp.int32)
        far_lists = (digits[0] * 256 + digits[1]).reshape(-1, kept)
        orders = jnp.stack([orders, exchange(orders, "grid", 2)], axis=1).reshape(-1, kept)
    else:
        near = exchange(near, "grid", 1)
    near = [near] + [exchange(m, "grid", 1) for m in mixing[1:]]

    def over_bands(block):
        blocks = [block]
        for t in reversed(range(1, band_bits)):
            blocks = blocks + [exchange(m, "band", 1 << t) for m in blocks]
        return blocks

    def joined(rows):
        return jnp.concatenate(over_bands(rows), axis=0)

    def over_cores(rows):
        return [rows, exchange(rows, "band", 1)]

    def shares(matrices):
        whole = jnp.concatenate(matrices, axis=1)
        return [half_of(whole, place & 1), exchange(half_of(whole, 1 - (place & 1)), "band", 1)]

    own = pick([block for p in range(parts) for block in blocks_of(p, 0)], [orders[k] for p in places for k in p])
    far = [None] * parts
    far[-1] = pick([raw[:, i * width : (i + 1) * width] for i in range(count)], [orders[k] for k in places[-1]])
    if parts > 1:
        far[0] = pick(blocks_of(0, 1), far_lists)
        far[0], near = lax.optimization_barrier((far[0], near))
        far[0] = exchange(far[0], "grid", 1)
    own = over_cores(joined(own))
    mixes = shares(mixing) + shares(near)

    def block_of(p, rows):
        columns = count * kept
        return [columns, [(array, p * columns) for array in own] + [(array, 0) for array in over_cores(rows)], []]

    go = block_of(parts - 1, joined(far[-1]))

    if parts > 1:
        stay = None
        for t in range(1, grid_bits):
            pieces = halves(go) if t < grid_bits - 1 else [go]
            codes = [sketch("code", piece, mixes).astype(f16) for piece in reversed(pieces)]
            got = exchange(codes[0], "grid", 1 << t)
            if stay is None:
                codes[1:], rows = lax.optimization_barrier((codes[1:], far[0]))
                got, rows = lax.optimization_barrier((got, joined(rows)))
                stay = block_of(0, rows)
            if len(pieces) > 1:
                stay, go = halves(stay)
                go[2].append((got.astype(f32), 0))
                stay[2].append((exchange(codes[1], "grid", 1 << t).astype(f32), 0))
        held = sketch("keep", stay, mixes)
        chosen = sketch("multiply", [kept, [], [(got.astype(f32), 0)]], mixes, [(held, 0)])
    else:
        chosen = sketch("multiply", go, mixes)

    def in_order(block, got, t):
        upper = place >> t & 1 == 1
        count = 1 << (band_bits - 1 - t)
        share = block.reshape((count, -1) + block.shape[1:])
        other = got.reshape(share.shape)
        low, high = jnp.where(upper, other, share), jnp.where(upper, share, other)
        return jnp.concatenate([low, high], axis=1).reshape((-1,) + block.shape[1:])

    def over_higher(block):
        for t in reversed(range(1, band_bits)):
            block = in_order(block, exchange(block, "band", 1 << t), t)
        return block

    rounds = grid_bits + 1
    paired = rounds - 2 + rounds % 2
    index = lax.broadcasted_iota(jnp.int32, (kept, kept), 0)
    even = place & 1 == 0
    shared, grams = [], []
    for section in range(rounds):
        if section:
            got = exchange(chosen, "grid", 1 << section - 1)
            upper = here >> section - 1 & 1
            mine = (index == order[section] - upper * kept).astype(bf16)
            other = (index == order[section] - (1 - upper) * kept).astype(bf16)
            chosen = jnp.dot(chosen, mine, preferred_element_type=f32) + jnp.dot(got, other, preferred_element_type=f32)
            chosen = chosen.astype(bf16)
        if section == rounds - 1:
            final = over_higher(chosen)
        else:
            block = chosen
            if shared:
                block, shared[-1] = lax.optimization_barrier((block, shared[-1]))
            shared.append(joined(block))
            if section < paired and section % 2:
                low, high = shared[-2:]
                got = exchange(jnp.where(even, high, low), "band", 1)
                grams.append(gram_of([jnp.where(even, low, high), got]))
    got = exchange(final, "band", 1)
    cands = in_order(final, got, 0)
    if rounds % 2:
        odd = log_pivots([gram_of([cands])])
        quality = jnp.where(even, 0.0, odd) + (log_pivots(grams) if grams else 0.0)
    else:
        last = gram_of([shared[-1], exchange(shared[-1], "band", 1)])
        quality = log_pivots(grams + [last], place, final, got)
    return cands, quality + exchange(quality, "band", 1)


def solution(mesh):
    in_specs = (
        P(("band", "grid"), None),
        P(("band", "grid"), None),
        P(("band", "grid"), None),
        P("grid", None, None),
    )
    out_specs = (P(), P("grid", None))
    return jax.shard_map(local, mesh=mesh, in_specs=in_specs, out_specs=out_specs, check_vma=False)
```
